32 devices in a mesh: section: 4 (over y, core), frame: 8 (over z, x).
Axes of the slice: x: 2, y: 2, z: 4, core: 2. Of those that a mesh axis runs over, the one named last changes fastest.
Arguments:
- newcomer_groups: bfloat16 [1, 2048, 1536], P(None, 'frame'), may hold values from -6 to 6
- pending_inputs: bfloat16 [4, 2048, 1536], P('section', 'frame'), may hold values from -6 to 6
- speaker_clip_ids: int32 [5, 2048], P(None, 'frame'), may hold values from 0 to 15, never falling along the last dimension, each value on 1 to 256 neighbouring positions
- selfattend_scaling: float32 [4, 1536], P('section'), may hold values from 0.1 to 1.9
- triple_projection_matrix: bfloat16 [4, 1536, 4608], P('section', 'frame'), may hold values from -1 to 1
- selfattend_final_matrix: bfloat16 [4, 1536, 1536], P('section', 'frame'), may hold values from -0.15625 to 0.15625
- depthwise_scaling: float32 [4, 1536], P('section'), may hold values from 0.1 to 1.9
- sigmoid_expand_matrix: bfloat16 [4, 1536, 3072], P('section', 'frame'), may hold values from -0.15625 to 0.15625
- filter_taps: float32 [4, 31, 1536], P('section'), may hold values from -1 to 1
- combine_channel_matrix: bfloat16 [4, 1536, 1536], P('section', 'frame'), may hold values from -0.15625 to 0.15625
Outputs:
- section_out: bfloat16 [2, 4, 2048, 1536], P(None, 'section', 'frame')
The draws below stay inside these ranges and needn't reach their ends.
Inputs may be any that keep to these rules, and one draw needn't show every extreme that they name: `speaker_clip_ids`: in every row the ids never fall along frames; every utterance has 1 to 256 frames, and one utterance of each row has exactly 256.
All inputs are finite; a program needn't handle non-finite values.
Results may differ from the reference program's by a relative error of at most 0.008.
Values may be sent and summed in bfloat16 or wider, within the bound.
No kernel may reach another device: no remote copies, remote signals or barrier semaphores. Data moves between devices by JAX's collectives and lax.ppermute only.
A program may use at most 192 MiB of HBM per device.

```python
import math
import jax
import jax.numpy as jnp
import numpy as np
from jax import lax

HIDDEN_FEATURE = 1536
HEADS = 24
HEAD_DIM = 64
KERNEL = 31
TOK_DEV = 256
TICKS = 2
HANDOFF_PARTS = 4
GROUP_SAMPLES = 2048
MB = 5
SEGS = 16
N_FRAME = 8


def draw_triple_projection_matrix(key, part):
    scale = HIDDEN_FEATURE ** (-0.5)
    base = jax.random.normal(key, (HANDOFF_PARTS, HIDDEN_FEATURE, 3 * HIDDEN_FEATURE), jnp.float32)
    base = jnp.clip(base, -6.0, 6.0) * scale
    return base.astype(jnp.bfloat16)


def steps_of(stream_key, extent, shards, smallest, top_value):
    def one(position, blocks):
        heights = jax.random.uniform(jax.random.fold_in(jax.random.fold_in(stream_key, 6), position), (blocks,), jnp.float32, smallest / len(shards), top_value / len(shards))
        return jnp.repeat(jnp.exp(heights), extent[position] // blocks).reshape((-1,) + (1,) * (len(extent) - position - 1))

    factor_of = one(*shards[0])
    for cut in shards[1:]:
        factor_of = factor_of * one(*cut)
    return factor_of


def profile(amount, total, bound, lean):
    portions = [(1 << 20) // math.isqrt(grade ** lean) + 1 for grade in range(2, amount + 1)]
    spare, given = total - bound - (amount - 1), [1] * (amount - 1)
    while spare > 0:
        free = [i for i in range(amount - 1) if given[i] < bound]
        mass, remaining = sum([portions[i] for i in free]), spare
        for i in free:
            extra = min(bound - given[i], max(1, remaining * portions[i] // mass), spare)
            given[i] = given[i] + extra
            spare = spare - extra
    return np.array([bound] + given)


def uneven(own_key, count, total, reach, slope):
    if count == 2:
        one = jax.random.randint(own_key, (), max(1, total - reach), min(reach, total - 1) + 1)
        return jnp.stack([one, total - one])
    sizes = jnp.asarray(profile(count, total, reach, slope), jnp.int32)
    couples = (count - 1) // 2
    donor, sink = sizes[1:1 + 2 * couples:2], sizes[2:2 + 2 * couples:2]
    slack = jnp.minimum(donor - 1, reach - sink)
    passed = jax.random.randint(jax.random.fold_in(own_key, 1), (couples,), 0, 1 << 20) % (slack + 1)
    sizes = sizes.at[1:1 + 2 * couples:2].set(donor - passed).at[2:2 + 2 * couples:2].set(sink + passed)
    return sizes[jax.random.permutation(jax.random.fold_in(own_key, 2), count)]


def bell_draw(key, shape, scale, limit, shards=(), kind=jnp.bfloat16):
    values = jax.random.normal(key, shape, jnp.float32) * scale
    if len(shards) > 0:
        values = steps_of(key, shape, shards, -0.22, 0.18) * values
    return jnp.clip(values, min=-limit, max=limit).astype(kind)


def setup_inputs(seed: int = 0) -> dict:
    streams_of = jax.random.split(jax.random.key(seed), 11)
    newcomer_groups = bell_draw(streams_of[0], (TICKS - 1, GROUP_SAMPLES, HIDDEN_FEATURE), 1.0, 6.0, ((1, 8),))
    pending_inputs = bell_draw(streams_of[1], (HANDOFF_PARTS, GROUP_SAMPLES, HIDDEN_FEATURE), 1.0, 6.0, ((0, 4), (1, 8)))
    speaker_clip_ids = jax.vmap(lambda own: jnp.searchsorted(jnp.cumsum(uneven(own, SEGS, GROUP_SAMPLES, TOK_DEV, 0)), jnp.arange(GROUP_SAMPLES), side="right"))(jax.random.split(streams_of[2], MB)).reshape((MB, GROUP_SAMPLES)).astype(jnp.int32)
    selfattend_scaling = jnp.clip(1.0 + 0.18 * jax.random.normal(streams_of[3], (HANDOFF_PARTS, HIDDEN_FEATURE), jnp.float32), 0.1, 1.9)
    triple_projection_matrix = draw_triple_projection_matrix(jax.random.fold_in(streams_of[10], 71), 0)
    selfattend_final_matrix = bell_draw(streams_of[5], (HANDOFF_PARTS, HIDDEN_FEATURE, HIDDEN_FEATURE), HIDDEN_FEATURE ** -0.5, 0.15625, ((0, 4), (1, 8)))
    depthwise_scaling = jnp.clip(1.0 + 0.18 * jax.random.normal(streams_of[6], (HANDOFF_PARTS, HIDDEN_FEATURE), jnp.float32), 0.1, 1.9)
    sigmoid_expand_matrix = bell_draw(streams_of[7], (HANDOFF_PARTS, HIDDEN_FEATURE, 2 * HIDDEN_FEATURE), HIDDEN_FEATURE ** -0.5, 0.15625, ((0, 4), (1, 8)))
    filter_taps = bell_draw(streams_of[8], (HANDOFF_PARTS, KERNEL, HIDDEN_FEATURE), KERNEL ** -0.5, 1.0, ((0, 4),), jnp.float32)
    combine_channel_matrix = bell_draw(streams_of[9], (HANDOFF_PARTS, HIDDEN_FEATURE, HIDDEN_FEATURE), HIDDEN_FEATURE ** -0.5, 0.15625, ((0, 4), (1, 8)))
    return dict(newcomer_groups=newcomer_groups, pending_inputs=pending_inputs, speaker_clip_ids=speaker_clip_ids, selfattend_scaling=selfattend_scaling, triple_projection_matrix=triple_projection_matrix, selfattend_final_matrix=selfattend_final_matrix, depthwise_scaling=depthwise_scaling, sigmoid_expand_matrix=sigmoid_expand_matrix, filter_taps=filter_taps, combine_channel_matrix=combine_channel_matrix)


EPS = 1e-05

def layer_norm(sample_lines, gain):
    mean = lax.optimization_barrier(jnp.mean(sample_lines, axis=-1, keepdims=True))
    centred = sample_lines - mean
    spread = lax.optimization_barrier(jnp.mean(centred * centred, axis=-1, keepdims=True))
    return centred * lax.rsqrt(spread + EPS) * gain

def attend_block(query, wide_keys, wide_values, seg_wide, seg_own):
    sample_lines = query.shape[0]
    shaped_q = query.astype(jnp.float32).reshape(sample_lines, HEADS, HEAD_DIM)
    shaped_k = wide_keys.astype(jnp.float32).reshape(wide_keys.shape[0], HEADS, HEAD_DIM)
    shaped_v = wide_values.astype(jnp.float32).reshape(wide_values.shape[0], HEADS, HEAD_DIM)
    scores = jnp.einsum('qhd,khd->hqk', shaped_q, shaped_k)
    allowed = (seg_own[:, None] == seg_wide[None, :])[None]
    scores = jnp.where(allowed, scores, -1e+30)
    top = lax.optimization_barrier(jnp.max(scores, axis=-1, keepdims=True))
    expd = jnp.exp(scores - top)
    probs = (expd / lax.optimization_barrier(jnp.sum(expd, axis=-1, keepdims=True))).astype(jnp.bfloat16)
    context = jnp.einsum('hqk,khd->qhd', probs.astype(jnp.float32), shaped_v)
    return context.astype(jnp.bfloat16).reshape(sample_lines, HIDDEN_FEATURE)

def depthwise(wide_glu, seg_conv, seg_own, taps):
    sample_lines = seg_own.shape[0]
    total = jnp.zeros((sample_lines, wide_glu.shape[1]), jnp.float32)
    for tap in range(taps.shape[0]):
        same = (seg_conv[tap:tap + sample_lines] == seg_own)[:, None]
        total = total + jnp.where(same, wide_glu[tap:tap + sample_lines].astype(jnp.float32) * taps[tap], 0.0)
    return total

def block(present_activity, seg, gain_a, wq, wo, gain_c, wg, taps, wm):
    resid = present_activity.astype(jnp.float32)
    normed = layer_norm(resid, gain_a).astype(jnp.bfloat16)
    projected = jnp.dot(normed, wq, preferred_element_type=jnp.float32)
    query = (projected[:, :HIDDEN_FEATURE] * HEAD_DIM ** (-0.5)).astype(jnp.bfloat16)
    keys = projected[:, HIDDEN_FEATURE:2 * HIDDEN_FEATURE].astype(jnp.bfloat16)
    values = projected[:, 2 * HIDDEN_FEATURE:].astype(jnp.bfloat16)
    empty = jnp.zeros((TOK_DEV, HIDDEN_FEATURE), jnp.bfloat16)
    keys_pad = jnp.concatenate([empty, keys, empty], axis=0)
    values_pad = jnp.concatenate([empty, values, empty], axis=0)
    outside = jnp.full((TOK_DEV,), -1, jnp.int32)
    seg_pad = jnp.concatenate([outside, seg.astype(jnp.int32), outside], axis=0)

    def one_block(index):
        start = (index * TOK_DEV).astype(jnp.int32)
        block_q = lax.dynamic_slice_in_dim(query, start, TOK_DEV, 0)
        block_k = lax.dynamic_slice_in_dim(keys_pad, start, 3 * TOK_DEV, 0)
        block_v = lax.dynamic_slice_in_dim(values_pad, start, 3 * TOK_DEV, 0)
        block_s = lax.dynamic_slice_in_dim(seg_pad, start, 3 * TOK_DEV, 0)
        own_s = lax.dynamic_slice_in_dim(seg.astype(jnp.int32), start, TOK_DEV, 0)
        return attend_block(block_q, block_k, block_v, block_s, own_s)
    context = lax.map(one_block, jnp.arange(N_FRAME, dtype=jnp.int32)).reshape(GROUP_SAMPLES, HIDDEN_FEATURE)
    resid = resid + jnp.dot(context, wo, preferred_element_type=jnp.float32)
    conv_in = layer_norm(resid, gain_c).astype(jnp.bfloat16)
    doubled = jnp.dot(conv_in, wg, preferred_element_type=jnp.float32)
    glu = (doubled[:, :HIDDEN_FEATURE] * jax.nn.sigmoid(doubled[:, HIDDEN_FEATURE:])).astype(jnp.bfloat16)
    half = KERNEL // 2
    rim = jnp.zeros((half, HIDDEN_FEATURE), jnp.bfloat16)
    glu_pad = jnp.concatenate([rim, glu, rim], axis=0)
    seg_rim = jnp.full((half,), -1, jnp.int32)
    seg_conv = jnp.concatenate([seg_rim, seg.astype(jnp.int32), seg_rim], axis=0)
    depth = depthwise(glu_pad, seg_conv, seg.astype(jnp.int32), taps)
    act = (depth * jax.nn.sigmoid(depth)).astype(jnp.bfloat16)
    resid = resid + jnp.dot(act, wm, preferred_element_type=jnp.float32)
    return resid.astype(jnp.bfloat16)

def reference(newcomer_groups, pending_inputs, speaker_clip_ids, selfattend_scaling, triple_projection_matrix, selfattend_final_matrix, depthwise_scaling, sigmoid_expand_matrix, filter_taps, combine_channel_matrix):
    present_activity = [pending_inputs[part_number] for part_number in range(HANDOFF_PARTS)]
    results = []
    for tick in range(TICKS):
        made = []
        for part_number in range(HANDOFF_PARTS):
            batch_index = HANDOFF_PARTS - 1 - part_number + tick
            made.append(block(present_activity[part_number], speaker_clip_ids[batch_index], selfattend_scaling[part_number], triple_projection_matrix[part_number], selfattend_final_matrix[part_number], depthwise_scaling[part_number], sigmoid_expand_matrix[part_number], filter_taps[part_number], combine_channel_matrix[part_number]))
        results.append(jnp.stack(made))
        if tick + 1 < TICKS:
            present_activity = [newcomer_groups[tick]] + made[:-1]
    return jnp.stack(results)
```

```python
import jax
import jax.numpy as jnp
from jax import lax
from jax.sharding import PartitionSpec as P

HEADS = 24
KERNEL = 31
EPS = 1e-05
EDGE = 16
AXES = ("section", "frame")


def layer_norm(sample_lines, gain):
    mean = jnp.mean(sample_lines, axis=-1, keepdims=True)
    centred = sample_lines - mean
    spread = jnp.mean(centred * centred, axis=-1, keepdims=True)
    return centred * lax.rsqrt(spread + EPS) * gain


class Layout:
    def __init__(self, sections, frames):
        self.sections, self.frames, self.half = sections, frames, frames // 2
        self.gray = [r ^ (r >> 1) for r in range(self.half)]
        if sorted(self.gray) != list(range(self.half)):
            self.gray = list(range(self.half))

    def flat(self, section, frame):
        return section * self.frames + frame

    def worker(self, section, block):
        pair, high = divmod(section, 2)
        return self.flat(2 * pair + block % 2, high * self.half + self.gray.index(block // 2))

    def each(self):
        return [(s, b) for s in range(self.sections) for b in range(self.frames)]

    def to_workers(self):
        return [(self.flat(s, b), self.worker(s, b)) for s, b in self.each()]

    def to_homes(self):
        return [(there, here) for here, there in self.to_workers()]

    def shifted(self, step):
        return [
            (self.worker(s, b), self.worker(s, b + step))
            for s, b in self.each()
            if 0 <= b + step < self.frames
        ]

    def relay(self):
        return [
            (self.worker(s, b), self.worker(s + 1, b)) for s, b in self.each() if s + 1 < self.sections
        ]

    def first(self):
        return [(self.flat(0, b), self.worker(0, b)) for b in range(self.frames)]

    def rows_to_half(self):
        moves = []
        for s, f in self.each():
            (pair, high), (core, rest) = divmod(s, 2), divmod(f, self.half)
            if core != high:
                moves.append((self.flat(s, f), self.flat(2 * pair + core, high * self.half + rest)))
        return moves

    def flipped(self, section_bit, frame_bits):
        return [(self.flat(s, f), self.flat(s ^ section_bit, f ^ frame_bits)) for s, f in self.each()]

    def diagonal(self):
        return [
            (self.flat(s, f), self.flat(s, f ^ (1 if s % 2 == f // self.half else 2)))
            for s, f in self.each()
        ]

    def groups(self):
        return [
            [self.flat(2 * k + c, h * self.half + r) for c in range(2) for r in range(self.half)]
            for k in range(self.sections // 2)
            for h in range(2)
        ]


def send(value, moves):
    return lax.ppermute(value, AXES, moves)


def gathered(layout, chunks):
    core = lax.axis_index("section") % 2
    rest = lax.axis_index("frame") % layout.half
    at_home = core == lax.axis_index("frame") // layout.half
    held = []
    for chunk in chunks:
        if held:
            chunk, held[-1] = lax.optimization_barrier((chunk, held[-1]))
        held.append(jnp.where(at_home, chunk, send(chunk, layout.rows_to_half())))
    if layout.half != 4:
        return [
            lax.all_gather(own, AXES, axis=0, tiled=True, axis_index_groups=layout.groups())
            for own in held
        ]
    pieces = []
    for own in held:
        cut = own.shape[1] // 2
        along_x = send(own, layout.flipped(0, 1))
        along_z = send(own, layout.flipped(0, 2))
        low = send(along_z[:, :cut], layout.flipped(0, 1))
        high = send(jnp.where(at_home, along_z[:, cut:], along_x[:, cut:]), layout.diagonal())
        pieces.append((own, along_x, along_z, jnp.concatenate([low, high], axis=1)))
    whole = []
    block = jnp.arange(8)
    order = jnp.where(block // 4 == core, 0, 4) + ((block % 4) ^ rest)
    for index, piece in enumerate(pieces):
        near = jnp.stack(piece)
        if index + 1 < len(pieces):
            near, _ = lax.optimization_barrier((near, pieces[index + 1][1]))
        far = send(near, layout.flipped(1, 0))
        both = jnp.concatenate([near, far], axis=0)
        whole.append(both[order].reshape(-1, both.shape[-1]))
    return whole


def attend(query, wide_keys, wide_values, seg_wide, seg_own):
    sample_lines, feature_count = query.shape
    head_dim = feature_count // HEADS
    shaped_q = query.reshape(sample_lines, HEADS, head_dim)
    shaped_k = wide_keys.reshape(wide_keys.shape[0], HEADS, head_dim)
    shaped_v = wide_values.reshape(wide_values.shape[0], HEADS, head_dim)
    scores = jnp.einsum("qhd,khd->hqk", shaped_q, shaped_k, preferred_element_type=jnp.float32)
    allowed = (seg_own[:, None] == seg_wide[None, :])[None]
    scores = jnp.where(allowed, scores, -1e30)
    top = jnp.max(scores, axis=-1, keepdims=True)
    expd = jnp.exp(scores - top)
    probs = (expd / jnp.sum(expd, axis=-1, keepdims=True)).astype(jnp.bfloat16)
    context = jnp.einsum("hqk,khd->qhd", probs, shaped_v, preferred_element_type=jnp.float32)
    return context.astype(jnp.bfloat16).reshape(sample_lines, feature_count)


def depthwise(wide_glu, seg_conv, seg_own, taps):
    sample_lines = seg_own.shape[0]
    total = jnp.zeros((sample_lines, wide_glu.shape[1]), jnp.float32)
    for tap in range(taps.shape[0]):
        same = (seg_conv[tap : tap + sample_lines] == seg_own)[:, None]
        total = total + jnp.where(
            same, wide_glu[tap : tap + sample_lines].astype(jnp.float32) * taps[tap], 0.0
        )
    return total


def tick_of(wide, seg_wide, weights, gains, taps):
    full_qkv, full_out, full_glu, full_mix = weights
    rows, width = wide.shape[0] // 3, wide.shape[1]
    start, stop = rows - EDGE, 2 * rows + EDGE
    half = KERNEL // 2
    resid = wide.astype(jnp.float32)
    normed = layer_norm(resid, gains[0]).astype(jnp.bfloat16)
    query = jnp.dot(normed[start:stop], full_qkv[:, :width], preferred_element_type=jnp.float32)
    query = (query * (width // HEADS) ** (-0.5)).astype(jnp.bfloat16)
    pair = jnp.dot(normed, full_qkv[:, width:], preferred_element_type=jnp.float32).astype(jnp.bfloat16)
    context = attend(query, pair[:, :width], pair[:, width:], seg_wide, seg_wide[start:stop])
    resid = resid[start:stop] + jnp.dot(context, full_out, preferred_element_type=jnp.float32)
    conv_in = layer_norm(resid, gains[1]).astype(jnp.bfloat16)
    doubled = jnp.dot(conv_in, full_glu, preferred_element_type=jnp.float32)
    glu = (doubled[:, :width] * jax.nn.sigmoid(doubled[:, width:])).astype(jnp.bfloat16)
    first = EDGE - half
    depth = depthwise(
        glu[first:], seg_wide[start + first : stop], seg_wide[rows : 2 * rows], taps
    )
    act = (depth * jax.nn.sigmoid(depth)).astype(jnp.bfloat16)
    resid = resid[EDGE : EDGE + rows] + jnp.dot(act, full_mix, preferred_element_type=jnp.float32)
    return resid.astype(jnp.bfloat16)


def on_device(
    layout,
    newcomer_groups,
    pending_inputs,
    speaker_clip_ids,
    selfattend_scaling,
    triple_projection_matrix,
    selfattend_final_matrix,
    depthwise_scaling,
    sigmoid_expand_matrix,
    filter_taps,
    combine_channel_matrix,
):
    rows, width = pending_inputs.shape[1:]
    sections, frames, half = layout.sections, layout.frames, layout.half
    core = lax.axis_index("section") % 2
    pair = lax.axis_index("section") // 2
    high = lax.axis_index("frame") // half
    rest = lax.axis_index("frame") % half
    section = 2 * pair + high
    block = 2 * jnp.asarray(layout.gray)[rest] + core
    ticks = newcomer_groups.shape[0] + 1

    present = send(pending_inputs[0], layout.to_workers())
    newcomers = [send(newcomer_groups[tick], layout.first()) for tick in range(ticks - 1)]
    ids = lax.all_gather(speaker_clip_ids + 1, "frame", axis=1, tiled=True)
    ids = jnp.pad(ids, ((0, 0), (rows, rows)))

    def small(value):
        other = send(value, layout.flipped(1, 0))
        return jnp.where(core == high, value, other)

    gains = (small(selfattend_scaling[0]), small(depthwise_scaling[0]))
    taps = small(filter_taps[0])
    joined = jnp.concatenate([selfattend_final_matrix[0], sigmoid_expand_matrix[0]], axis=1)
    full_qkv, full_joined, full_mix = gathered(
        layout, [triple_projection_matrix[0], joined, combine_channel_matrix[0]]
    )
    weights = (full_qkv, full_joined[:, :width], full_joined[:, width:], full_mix)
    made_all = []
    for tick in range(ticks):
        batch = sections - 1 - section + tick
        seg_wide = lax.dynamic_slice(ids, (batch, block * rows), (1, 3 * rows))[0]
        low = send(present, layout.shifted(1))
        up = send(present, layout.shifted(-1))
        wide = jnp.concatenate([low, present, up], axis=0)
        made = tick_of(wide, seg_wide, weights, gains, taps)
        made_all.append(send(made, layout.to_homes()))
        if tick + 1 < ticks:
            arrived = send(made, layout.relay())
            present = jnp.where(section == 0, newcomers[tick], arrived)
    return jnp.stack(made_all)[:, None]


def solution(mesh):
    layout = Layout(mesh.shape["section"], mesh.shape["frame"])
    in_specs = (
        P(None, "frame", None),
        P("section", "frame", None),
        P(None, "frame"),
        P("section", None),
        P("section", "frame", None),
        P("section", "frame", None),
        P("section", None),
        P("section", "frame", None),
        P("section", None, None),
        P("section", "frame", None),
    )
    out_specs = P(None, "section", "frame", None)

    def local(*args):
        return on_device(layout, *args)

    return jax.shard_map(
        local, mesh=mesh, in_specs=in_specs, out_specs=out_specs, check_vma=False
    )
```

```python
import functools

import jax
import jax.numpy as jnp
from jax import lax
from jax.experimental import pallas as pl
from jax.experimental.pallas import tpu as pltpu
from jax.sharding import PartitionSpec as P

HEADS = 24
KERNEL = 31
EPS = 1e-05
EDGE = 16
GROUP = 32
VMEM_BYTES = 56 * 1024 * 1024
AXES = ("section", "frame")


class Layout:
    def __init__(self, sections, frames):
        self.sections, self.frames, self.half = sections, frames, frames // 2
        self.gray = [r ^ (r >> 1) for r in range(self.half)]
        if sorted(self.gray) != list(range(self.half)):
            self.gray = list(range(self.half))

    def flat(self, section, frame):
        return section * self.frames + frame

    def worker(self, section, block):
        pair, high = divmod(section, 2)
        return self.flat(2 * pair + block % 2, high * self.half + self.gray.index(block // 2))

    def each(self):
        return [(s, b) for s in range(self.sections) for b in range(self.frames)]

    def to_workers(self, step=0):
        return [
            (self.flat(s, b + step), self.worker(s, b))
            for s, b in self.each()
            if 0 <= b + step < self.frames
        ]

    def to_homes(self):
        return [(there, here) for here, there in self.to_workers()]

    def shifted(self, step):
        return [
            (self.worker(s, b), self.worker(s, b + step))
            for s, b in self.each()
            if 0 <= b + step < self.frames
        ]

    def relay(self):
        return [
            (self.worker(s, b), self.worker(s + 1, b)) for s, b in self.each() if s + 1 < self.sections
        ]

    def first(self):
        return [(self.flat(0, b), self.worker(0, b)) for b in range(self.frames)]

    def rows_to_half(self):
        moves = []
        for s, f in self.each():
            (pair, high), (core, rest) = divmod(s, 2), divmod(f, self.half)
            if core != high:
                moves.append((self.flat(s, f), self.flat(2 * pair + core, high * self.half + rest)))
        return moves

    def flipped(self, section_bit, frame_bits):
        return [(self.flat(s, f), self.flat(s ^ section_bit, f ^ frame_bits)) for s, f in self.each()]

    def diagonal(self):
        return [
            (self.flat(s, f), self.flat(s, f ^ (1 if s % 2 == f // self.half else 2)))
            for s, f in self.each()
        ]

    def groups(self):
        return [
            [self.flat(2 * k + c, h * self.half + r) for c in range(2) for r in range(self.half)]
            for k in range(self.sections // 2)
            for h in range(2)
        ]


def send(value, moves):
    return lax.ppermute(value, AXES, moves)


def gathered(layout, chunks):
    core = lax.axis_index("section") % 2
    rest = lax.axis_index("frame") % layout.half
    at_home = core == lax.axis_index("frame") // layout.half
    held = []
    for chunk in chunks:
        if held:
            chunk, held[-1] = lax.optimization_barrier((chunk, held[-1]))
        held.append(jnp.where(at_home, chunk, send(chunk, layout.rows_to_half())))
    if layout.half != 4:
        whole = [
            lax.all_gather(own, AXES, axis=0, tiled=True, axis_index_groups=layout.groups())
            for own in held
        ]
        return [(one[None],) for one in whole], jnp.zeros((1,), jnp.int32)
    pieces = []
    for own in held:
        half = own.shape[1] // 2
        along_x = send(own, layout.flipped(0, 1))
        along_z = send(own, layout.flipped(0, 2))
        low = send(along_z[:, :half], layout.flipped(0, 1))
        high = send(jnp.where(at_home, along_z[:, half:], along_x[:, half:]), layout.diagonal())
        pieces.append((own, along_x, along_z, jnp.concatenate([low, high], axis=1)))
    whole = []
    for index, piece in enumerate(pieces):
        near = jnp.stack(piece)
        if index + 1 < len(pieces):
            near, _ = lax.optimization_barrier((near, pieces[index + 1][1]))
        whole.append((near, send(near, layout.flipped(1, 0))))
    near_place = core * 4 + (jnp.arange(4) ^ rest)
    place = jnp.concatenate([near_place, near_place ^ 4])
    return whole, place.astype(jnp.int32) * chunks[0].shape[0]


def cut(total, most):
    return max(w for w in range(128, most + 1, 128) if total % w == 0)


def load_columns(offsets, pieces, target, columns, sem):
    place = 0
    for piece in pieces:
        count, height = piece.shape[:2]
        for index in range(count):
            row = pl.multiple_of(offsets[place], 16)
            place += 1
            pltpu.make_async_copy(
                piece.at[index, :, columns], target.at[pl.ds(row, height), columns], sem
            ).start()


def await_columns(target, columns, sem):
    pltpu.make_async_copy(target.at[:, columns], target.at[:, columns], sem).wait()


def normalised(lines, gain):
    mean = jnp.mean(lines, axis=-1, keepdims=True)
    centred = lines - mean
    spread = jnp.mean(centred * centred, axis=-1, keepdims=True)
    return (centred * lax.rsqrt(spread + EPS) * gain).astype(jnp.bfloat16)


def attention_kernel(
    pieces, offsets, low, own, up, gain, seg_rows, seg_keys, *rest
):
    weight, (context, matrix, normed, query, keys, values, bias, sems) = rest[:pieces], rest[pieces:]
    rows, width = own.shape
    wide, start, queries = 3 * rows, rows - EDGE, rows + 2 * EDGE
    step = cut(width, 768)
    spans = [pl.ds(at, step) for at in range(0, 3 * width, step)]
    for index, span in enumerate(spans):
        load_columns(offsets, weight, matrix, span, sems.at[index])
    for index, block in enumerate((low, own, up)):
        normed[pl.ds(index * rows, rows), :] = normalised(block[...].astype(jnp.float32), gain[...])
    tile, window = queries // 2, 2 * rows + 128
    firsts = (0, wide - window)
    for part in range(2):
        same = seg_rows[pl.ds(part * tile, tile), :] == seg_keys[:, pl.ds(firsts[part], window)]
        sheet = jnp.where(same, 0.0, -1e30)
        bias[part, pl.ds(0, tile), :] = sheet
        bias[part, pl.ds(tile, tile), :] = sheet
    per = width // step
    for index, span in enumerate(spans):
        await_columns(matrix, span, sems.at[index])
        kind, at = divmod(index, per)
        place = pl.ds(at * step, step)
        if kind == 0:
            made = jnp.dot(
                normed[pl.ds(start, queries), :], matrix[:, span], preferred_element_type=jnp.float32
            )
            query[:, place] = (made * (width // HEADS) ** (-0.5)).astype(jnp.bfloat16)
        else:
            made = jnp.dot(normed[...], matrix[:, span], preferred_element_type=jnp.float32)
            (keys if kind == 1 else values)[:, place] = made.astype(jnp.bfloat16)

    head = width // HEADS
    together = 128 // head
    lanes = lax.broadcasted_iota(jnp.int32, (tile, 128), 1) // head

    def heads(index, carry):
        place = pl.ds(pl.multiple_of(index * 128, 128), 128)
        for part in range(2):
            asked = query[pl.ds(part * tile, tile), place]
            stacked = jnp.concatenate(
                [jnp.where(lanes == one, asked, jnp.zeros_like(asked)) for one in range(together)], axis=0
            )
            seen = pl.ds(firsts[part], window)
            scores = lax.dot_general(
                stacked, keys[seen, place], (((1,), (1,)), ((), ())), preferred_element_type=jnp.float32
            )
            scores = scores + bias[part]
            expd = jnp.exp(scores - jnp.max(scores, axis=-1, keepdims=True))
            share = 1.0 / jnp.sum(expd, axis=-1, keepdims=True)
            mixed = jnp.dot(
                expd.astype(jnp.bfloat16), values[seen, place], preferred_element_type=jnp.float32
            ) * share
            result = mixed[:tile]
            for one in range(1, together):
                result = jnp.where(lanes == one, mixed[one * tile : (one + 1) * tile], result)
            context[pl.ds(part * tile, tile), place] = result.astype(jnp.bfloat16)
        return carry

    lax.fori_loop(0, width // 128, heads, 0)


def attention(offsets, weight, low, own, up, gain, seg_wide):
    rows, width = own.shape
    wide, queries = 3 * rows, rows + 2 * EDGE
    spans = 3 * width // cut(width, 768)
    whole = pl.BlockSpec(memory_space=pltpu.VMEM)
    seg_rows = seg_wide[rows - EDGE : 2 * rows + EDGE][:, None]
    return pl.pallas_call(
        functools.partial(attention_kernel, len(weight)),
        out_shape=jax.ShapeDtypeStruct((queries, width), jnp.bfloat16),
        in_specs=[pl.BlockSpec(memory_space=pltpu.SMEM)]
        + [whole] * 6
        + [pl.BlockSpec(memory_space=pl.ANY)] * len(weight),
        out_specs=whole,
        scratch_shapes=[
            pltpu.VMEM((width, 3 * width), jnp.bfloat16),
            pltpu.VMEM((wide, width), jnp.bfloat16),
            pltpu.VMEM((queries, width), jnp.bfloat16),
            pltpu.VMEM((wide, width), jnp.bfloat16),
            pltpu.VMEM((wide, width), jnp.bfloat16),
            pltpu.VMEM((2, queries, 2 * rows + 128), jnp.float32),
            pltpu.SemaphoreType.DMA((spans,)),
        ],
        compiler_params=pltpu.CompilerParams(vmem_limit_bytes=VMEM_BYTES),
        cost_estimate=pl.CostEstimate(
            flops=2 * width * width * (queries + 2 * wide) + 4 * queries * wide * width,
            bytes_accessed=6 * width * width + 8 * rows * width,
            transcendentals=HEADS * queries * wide,
        ),
        name="attention",
    )(offsets, low, own, up, gain, seg_rows, seg_wide[None, :], *weight)


def convolution_kernel(
    pieces, offsets, context, low, own, up, gain, seg_rows, masks_seg, taps, *rest
):
    weight = rest[:pieces]
    act, resid_out, matrix, resid, conv_in, gated, moved, masks, sems = rest[pieces:]
    rows, width = own.shape
    queries = rows + 2 * EDGE
    step = cut(width, 512)
    count = width // step
    outs = [pl.ds(at * step, step) for at in range(count)]
    values = [pl.ds(width + at * step, step) for at in range(count)]
    gates = [pl.ds(2 * width + at * step, step) for at in range(count)]
    order = outs + [span for both in zip(values, gates) for span in both]
    for index, span in enumerate(order):
        load_columns(offsets, weight, matrix, span, sems.at[index])
    half = KERNEL // 2
    for tap in range(KERNEL):
        same = masks_seg[:, tap : tap + 1] == seg_rows[...]
        masks[tap] = jnp.broadcast_to(jnp.where(same, 1.0, 0.0), (rows, 128))
    for index, span in enumerate(outs):
        await_columns(matrix, span, sems.at[index])
        added = jnp.dot(context[...], matrix[:, span], preferred_element_type=jnp.float32)
        resid[pl.ds(0, EDGE), span] = added[:EDGE] + low[pl.ds(rows - EDGE, EDGE), span].astype(jnp.float32)
        resid[pl.ds(EDGE, rows), span] = added[EDGE : EDGE + rows] + own[:, span].astype(jnp.float32)
        resid[pl.ds(EDGE + rows, EDGE), span] = added[EDGE + rows :] + up[pl.ds(0, EDGE), span].astype(
            jnp.float32
        )
    conv_in[...] = normalised(resid[...], gain[...])
    resid_out[...] = resid[pl.ds(EDGE, rows), :]
    for index in range(count):
        await_columns(matrix, values[index], sems.at[count + 2 * index])
        await_columns(matrix, gates[index], sems.at[count + 2 * index + 1])
        value = jnp.dot(conv_in[...], matrix[:, values[index]], preferred_element_type=jnp.float32)
        gate = jnp.dot(conv_in[...], matrix[:, gates[index]], preferred_element_type=jnp.float32)
        glu = (value * jax.nn.sigmoid(gate)).astype(jnp.bfloat16).astype(jnp.float32)
        gated[pl.ds(0, queries), :] = glu
        for shift in range(8):
            moved[shift] = gated[pl.ds(shift, queries), :]

        def lines(group, carry):
            at = pl.multiple_of(group * GROUP, GROUP)
            for lane in range(0, step, 128):
                total = jnp.zeros((GROUP, 128), jnp.float32)
                place = index * step + lane
                for tap in range(KERNEL):
                    first = EDGE - half + tap
                    part = moved[first % 8, pl.ds(at + first // 8 * 8, GROUP), lane : lane + 128]
                    part = part * masks[tap, pl.ds(at, GROUP), :]
                    total = total + part * taps[tap : tap + 1, place : place + 128]
                act[pl.ds(at, GROUP), place : place + 128] = (total * jax.nn.sigmoid(total)).astype(
                    jnp.bfloat16
                )
            return carry

        lax.fori_loop(0, rows // GROUP, lines, 0)


def convolution(offsets, weight, context, low, own, up, gain, seg_wide, taps):
    rows, width = own.shape
    queries = rows + 2 * EDGE
    step = cut(width, 512)
    whole = pl.BlockSpec(memory_space=pltpu.VMEM)
    first = rows - KERNEL // 2
    seg_taps = jnp.stack([seg_wide[first + tap : first + tap + rows] for tap in range(KERNEL)], axis=1)
    return pl.pallas_call(
        functools.partial(convolution_kernel, len(weight)),
        out_shape=(
            jax.ShapeDtypeStruct((rows, width), jnp.bfloat16),
            jax.ShapeDtypeStruct((rows, width), jnp.float32),
        ),
        in_specs=[pl.BlockSpec(memory_space=pltpu.SMEM)]
        + [whole] * 8
        + [pl.BlockSpec(memory_space=pl.ANY)] * len(weight),
        out_specs=(whole, whole),
        scratch_shapes=[
            pltpu.VMEM((width, 3 * width), jnp.bfloat16),
            pltpu.VMEM((queries, width), jnp.float32),
            pltpu.VMEM((queries, width), jnp.bfloat16),
            pltpu.VMEM((queries + 8, step), jnp.float32),
            pltpu.VMEM((8, queries, step), jnp.float32),
            pltpu.VMEM((KERNEL, rows, 128), jnp.float32),
            pltpu.SemaphoreType.DMA((3 * width // step,)),
        ],
        compiler_params=pltpu.CompilerParams(vmem_limit_bytes=VMEM_BYTES),
        cost_estimate=pl.CostEstimate(
            flops=6 * width * width * queries + 3 * KERNEL * rows * width,
            bytes_accessed=6 * width * width + 8 * rows * width,
            transcendentals=2 * rows * width,
        ),
        name="convolution",
    )(
        offsets, context, low, own, up, gain, seg_wide[rows : 2 * rows][:, None], seg_taps, taps, *weight
    )


def mixing_kernel(pieces, offsets, act, resid, *rest):
    weight, (out, matrix, sems) = rest[:pieces], rest[pieces:]
    width = act.shape[1]
    step = cut(width, 512)
    spans = [pl.ds(at, step) for at in range(0, width, step)]
    for index, span in enumerate(spans):
        load_columns(offsets, weight, matrix, span, sems.at[index])
    for index, span in enumerate(spans):
        await_columns(matrix, span, sems.at[index])
        made = jnp.dot(act[...], matrix[:, span], preferred_element_type=jnp.float32)
        out[:, span] = (resid[:, span] + made).astype(jnp.bfloat16)


def mixing(offsets, weight, act, resid):
    rows, width = act.shape
    whole = pl.BlockSpec(memory_space=pltpu.VMEM)
    return pl.pallas_call(
        functools.partial(mixing_kernel, len(weight)),
        out_shape=jax.ShapeDtypeStruct((rows, width), jnp.bfloat16),
        in_specs=[pl.BlockSpec(memory_space=pltpu.SMEM)]
        + [whole] * 2
        + [pl.BlockSpec(memory_space=pl.ANY)] * len(weight),
        out_specs=whole,
        scratch_shapes=[
            pltpu.VMEM((width, width), jnp.bfloat16),
            pltpu.SemaphoreType.DMA((width // cut(width, 512),)),
        ],
        compiler_params=pltpu.CompilerParams(vmem_limit_bytes=VMEM_BYTES),
        cost_estimate=pl.CostEstimate(
            flops=2 * width * width * rows, bytes_accessed=2 * width * width + 8 * rows * width, transcendentals=0
        ),
        name="mixing",
    )(offsets, act, resid, *weight)


def on_device(
    layout,
    newcomer_groups,
    pending_inputs,
    speaker_clip_ids,
    selfattend_scaling,
    triple_projection_matrix,
    selfattend_final_matrix,
    depthwise_scaling,
    sigmoid_expand_matrix,
    filter_taps,
    combine_channel_matrix,
):
    core = lax.axis_index("section") % 2
    high = lax.axis_index("frame") // layout.half
    section = lax.axis_index("section") // 2 * 2 + high
    sections = layout.sections
    ticks = newcomer_groups.shape[0] + 1

    present = send(pending_inputs[0], layout.to_workers())
    newcomers = [send(newcomer_groups[tick], layout.first()) for tick in range(ticks - 1)]
    ids = jnp.concatenate(
        [send(speaker_clip_ids + 1, layout.to_workers(step)) for step in (-1, 0, 1)], axis=1
    )

    def small(value):
        other = send(value, layout.flipped(1, 0))
        return jnp.where(core == high, value, other)

    gain_a, gain_c = small(selfattend_scaling), small(depthwise_scaling)
    taps = small(filter_taps[0])
    joined = jnp.concatenate([selfattend_final_matrix[0], sigmoid_expand_matrix[0]], axis=1)
    (qkv, out_glu, mix), offsets = gathered(
        layout, [triple_projection_matrix[0], joined, combine_channel_matrix[0]]
    )
    made_all = []
    for tick in range(ticks):
        batch = sections - 1 - section + tick
        seg_wide = lax.dynamic_index_in_dim(ids, batch, 0, keepdims=False)
        low = send(present, layout.shifted(1))
        up = send(present, layout.shifted(-1))
        context = attention(offsets, qkv, low, present, up, gain_a, seg_wide)
        act, resid = convolution(offsets, out_glu, context, low, present, up, gain_c, seg_wide, taps)
        made = mixing(offsets, mix, act, resid)
        made_all.append(send(made, layout.to_homes()))
        if tick + 1 < ticks:
            arrived = send(made, layout.relay())
            present = jnp.where(section == 0, newcomers[tick], arrived)
    return jnp.stack(made_all)[:, None]


def solution(mesh):
    layout = Layout(mesh.shape["section"], mesh.shape["frame"])
    in_specs = (
        P(None, "frame", None),
        P("section", "frame", None),
        P(None, "frame"),
        P("section", None),
        P("section", "frame", None),
        P("section", "frame", None),
        P("section", None),
        P("section", "frame", None),
        P("section", None, None),
        P("section", "frame", None),
    )
    out_specs = P(None, "section", "frame", None)

    def local(*args):
        return on_device(layout, *args)

    return jax.shard_map(
        local, mesh=mesh, in_specs=in_specs, out_specs=out_specs, check_vma=False
    )
```

```python
import functools

import jax
import jax.numpy as jnp
from jax import lax
from jax.experimental import pallas as pl
from jax.experimental.pallas import tpu as pltpu
from jax.sharding import PartitionSpec as P

HEADS = 24
KERNEL = 31
EPS = 1e-05
EDGE = 16
GROUP = 32
VMEM_BYTES = 56 * 1024 * 1024
AXES = ("section", "frame")


class Layout:
    def __init__(self, sections, frames):
        self.sections, self.frames, self.half = sections, frames, frames // 2
        self.gray = [r ^ (r >> 1) for r in range(self.half)]
        if sorted(self.gray) != list(range(self.half)):
            self.gray = list(range(self.half))

    def flat(self, section, frame):
        return section * self.frames + frame

    def worker(self, section, block):
        pair, high = divmod(section, 2)
        return self.flat(2 * pair + block % 2, high * self.half + self.gray.index(block // 2))

    def each(self):
        return [(s, b) for s in range(self.sections) for b in range(self.frames)]

    def to_workers(self, step=0):
        return [
            (self.flat(s, b + step), self.worker(s, b))
            for s, b in self.each()
            if 0 <= b + step < self.frames
        ]

    def to_homes(self):
        return [(there, here) for here, there in self.to_workers()]

    def shifted(self, step):
        return [
            (self.worker(s, b), self.worker(s, b + step))
            for s, b in self.each()
            if 0 <= b + step < self.frames
        ]

    def relay(self):
        return [
            (self.worker(s, b), self.worker(s + 1, b)) for s, b in self.each() if s + 1 < self.sections
        ]

    def first(self):
        return [(self.flat(0, b), self.worker(0, b)) for b in range(self.frames)]

    def rows_to_half(self):
        moves = []
        for s, f in self.each():
            (pair, high), (core, rest) = divmod(s, 2), divmod(f, self.half)
            if core != high:
                moves.append((self.flat(s, f), self.flat(2 * pair + core, high * self.half + rest)))
        return moves

    def flipped(self, section_bit, frame_bits):
        return [(self.flat(s, f), self.flat(s ^ section_bit, f ^ frame_bits)) for s, f in self.each()]

    def diagonal(self):
        return [
            (self.flat(s, f), self.flat(s, f ^ (1 if s % 2 == f // self.half else 2)))
            for s, f in self.each()
        ]

    def groups(self):
        return [
            [self.flat(2 * k + c, h * self.half + r) for c in range(2) for r in range(self.half)]
            for k in range(self.sections // 2)
            for h in range(2)
        ]


def send(value, moves):
    return lax.ppermute(value, AXES, moves)


def behind(value, *earlier):
    return lax.optimization_barrier((value, earlier))[0]


class Weights:
    def __init__(self, layout):
        self.layout = layout
        self.core = lax.axis_index("section") % 2
        self.rest = lax.axis_index("frame") % layout.half
        self.at_home = self.core == lax.axis_index("frame") // layout.half
        self.tree = layout.half == 4

    def to_half(self, chunk):
        return jnp.where(self.at_home, chunk, send(chunk, self.layout.rows_to_half()))

    def to_sides(self, own):
        if not self.tree:
            return own, own
        return send(own, self.layout.flipped(0, 1)), send(own, self.layout.flipped(0, 2))

    def to_diagonal(self, along_x, along_z):
        if not self.tree:
            return along_x, along_z
        half = along_x.shape[1] // 2
        low = send(along_z[:, :half], self.layout.flipped(0, 1))
        high = jnp.where(self.at_home, along_z[:, half:], along_x[:, half:])
        return low, send(high, self.layout.diagonal())

    def offsets(self, rows):
        if not self.tree:
            return jnp.zeros((1,), jnp.int32)
        near = self.core * 4 + (jnp.arange(4) ^ self.rest)
        return jnp.concatenate([near, near ^ 4]).astype(jnp.int32) * rows

    def whole(self, own, sides, diagonal, *earlier):
        if not self.tree:
            whole = lax.all_gather(
                own, AXES, axis=0, tiled=True, axis_index_groups=self.layout.groups()
            )
            return (whole[None],)
        own, sides, diagonal = behind((own, sides, diagonal), *earlier)
        near = jnp.stack([own, *sides, jnp.concatenate(diagonal, axis=1)])
        return near, send(near, self.layout.flipped(1, 0))


def cut(total, most):
    return max(w for w in range(128, most + 1, 128) if total % w == 0)


def load_columns(offsets, pieces, target, columns, sem):
    place = 0
    for piece in pieces:
        count, height = piece.shape[:2]
        for index in range(count):
            row = pl.multiple_of(offsets[place], 16)
            place += 1
            pltpu.make_async_copy(
                piece.at[index, :, columns], target.at[pl.ds(row, height), columns], sem
            ).start()


def await_columns(target, columns, sem):
    pltpu.make_async_copy(target.at[:, columns], target.at[:, columns], sem).wait()


def normalised(lines, gain):
    mean = jnp.mean(lines, axis=-1, keepdims=True)
    centred = lines - mean
    spread = jnp.mean(centred * centred, axis=-1, keepdims=True)
    return (centred * lax.rsqrt(spread + EPS) * gain).astype(jnp.bfloat16)


def attention_kernel(
    pieces, offsets, low, own, up, gain, seg_rows, seg_keys, *rest
):
    weight, (context, matrix, normed, query, keys, values, bias, sems) = rest[:pieces], rest[pieces:]
    queries, width = context.shape
    rows = queries - 2 * EDGE
    wide, start = 3 * rows, rows - EDGE
    step = cut(width, 768)
    spans = [pl.ds(at, step) for at in range(0, 3 * width, step)]
    for index, span in enumerate(spans):
        load_columns(offsets, weight, matrix, span, sems.at[index])
    for index, block in enumerate((low, own, up)):
        normed[pl.ds(index * rows, rows), :] = normalised(
            block[pl.ds(0, rows), :].astype(jnp.float32), gain[...]
        )
    tile, window = queries // 2, 2 * rows + 128
    firsts = (0, wide - window)
    for part in range(2):
        same = seg_rows[pl.ds(part * tile, tile), :] == seg_keys[:, pl.ds(firsts[part], window)]
        sheet = jnp.where(same, 0.0, -1e30)
        bias[part, pl.ds(0, tile), :] = sheet
        bias[part, pl.ds(tile, tile), :] = sheet
    per = width // step
    for index, span in enumerate(spans):
        await_columns(matrix, span, sems.at[index])
        kind, at = divmod(index, per)
        place = pl.ds(at * step, step)
        if kind == 0:
            made = jnp.dot(
                normed[pl.ds(start, queries), :], matrix[:, span], preferred_element_type=jnp.float32
            )
            query[:, place] = (made * (width // HEADS) ** (-0.5)).astype(jnp.bfloat16)
        else:
            made = jnp.dot(normed[...], matrix[:, span], preferred_element_type=jnp.float32)
            (keys if kind == 1 else values)[:, place] = made.astype(jnp.bfloat16)

    head = width // HEADS
    together = 128 // head
    lanes = lax.broadcasted_iota(jnp.int32, (tile, 128), 1) // head

    def heads(index, carry):
        place = pl.ds(pl.multiple_of(index * 128, 128), 128)
        for part in range(2):
            asked = query[pl.ds(part * tile, tile), place]
            stacked = jnp.concatenate(
                [jnp.where(lanes == one, asked, jnp.zeros_like(asked)) for one in range(together)], axis=0
            )
            seen = pl.ds(firsts[part], window)
            scores = lax.dot_general(
                stacked, keys[seen, place], (((1,), (1,)), ((), ())), preferred_element_type=jnp.float32
            )
            scores = scores + bias[part]
            expd = jnp.exp(scores - jnp.max(scores, axis=-1, keepdims=True))
            share = 1.0 / jnp.sum(expd, axis=-1, keepdims=True)
            mixed = jnp.dot(
                expd.astype(jnp.bfloat16), values[seen, place], preferred_element_type=jnp.float32
            ) * share
            result = mixed[:tile]
            for one in range(1, together):
                result = jnp.where(lanes == one, mixed[one * tile : (one + 1) * tile], result)
            context[pl.ds(part * tile, tile), place] = result.astype(jnp.bfloat16)
        return carry

    lax.fori_loop(0, width // 128, heads, 0)


def attention(offsets, weight, low, own, up, gain, seg_wide):
    rows, width = seg_wide.shape[0] // 3, own.shape[1]
    wide, queries = 3 * rows, rows + 2 * EDGE
    spans = 3 * width // cut(width, 768)
    whole = pl.BlockSpec(memory_space=pltpu.VMEM)
    seg_rows = seg_wide[rows - EDGE : 2 * rows + EDGE][:, None]
    return pl.pallas_call(
        functools.partial(attention_kernel, len(weight)),
        out_shape=jax.ShapeDtypeStruct((queries, width), jnp.bfloat16),
        in_specs=[pl.BlockSpec(memory_space=pltpu.SMEM)]
        + [whole] * 6
        + [pl.BlockSpec(memory_space=pl.ANY)] * len(weight),
        out_specs=whole,
        scratch_shapes=[
            pltpu.VMEM((width, 3 * width), jnp.bfloat16),
            pltpu.VMEM((wide, width), jnp.bfloat16),
            pltpu.VMEM((queries, width), jnp.bfloat16),
            pltpu.VMEM((wide, width), jnp.bfloat16),
            pltpu.VMEM((wide, width), jnp.bfloat16),
            pltpu.VMEM((2, queries, 2 * rows + 128), jnp.float32),
            pltpu.SemaphoreType.DMA((spans,)),
        ],
        compiler_params=pltpu.CompilerParams(vmem_limit_bytes=VMEM_BYTES),
        cost_estimate=pl.CostEstimate(
            flops=2 * width * width * (queries + 2 * wide) + 4 * queries * wide * width,
            bytes_accessed=6 * width * width + 8 * rows * width,
            transcendentals=HEADS * queries * wide,
        ),
        name="attention",
    )(offsets, low, own, up, gain, seg_rows, seg_wide[None, :], *weight)


def convolution_kernel(
    pieces, offsets, context, low, own, up, gain, seg_rows, masks_seg, taps, *rest
):
    weight = rest[:pieces]
    act, resid_out, matrix, resid, conv_in, gated, moved, masks, sems = rest[pieces:]
    rows, width = act.shape
    queries = rows + 2 * EDGE
    step = cut(width, 512)
    count = width // step
    outs = [pl.ds(at * step, step) for at in range(count)]
    values = [pl.ds(width + at * step, step) for at in range(count)]
    gates = [pl.ds(2 * width + at * step, step) for at in range(count)]
    order = outs + [span for both in zip(values, gates) for span in both]
    for index, span in enumerate(order):
        load_columns(offsets, weight, matrix, span, sems.at[index])
    half = KERNEL // 2
    for tap in range(KERNEL):
        same = masks_seg[:, tap : tap + 1] == seg_rows[...]
        masks[tap] = jnp.broadcast_to(jnp.where(same, 1.0, 0.0), (rows, 128))
    for index, span in enumerate(outs):
        await_columns(matrix, span, sems.at[index])
        added = jnp.dot(context[...], matrix[:, span], preferred_element_type=jnp.float32)
        resid[pl.ds(0, EDGE), span] = added[:EDGE] + low[pl.ds(rows - EDGE, EDGE), span].astype(jnp.float32)
        resid[pl.ds(EDGE, rows), span] = added[EDGE : EDGE + rows] + own[pl.ds(0, rows), span].astype(jnp.float32)
        resid[pl.ds(EDGE + rows, EDGE), span] = added[EDGE + rows :] + up[pl.ds(0, EDGE), span].astype(
            jnp.float32
        )
    conv_in[...] = normalised(resid[...], gain[...])
    resid_out[...] = resid[pl.ds(EDGE, rows), :]
    for index in range(count):
        await_columns(matrix, values[index], sems.at[count + 2 * index])
        await_columns(matrix, gates[index], sems.at[count + 2 * index + 1])
        value = jnp.dot(conv_in[...], matrix[:, values[index]], preferred_element_type=jnp.float32)
        gate = jnp.dot(conv_in[...], matrix[:, gates[index]], preferred_element_type=jnp.float32)
        glu = (value * jax.nn.sigmoid(gate)).astype(jnp.bfloat16).astype(jnp.float32)
        gated[pl.ds(0, queries), :] = glu
        for shift in range(8):
            moved[shift] = gated[pl.ds(shift, queries), :]

        def lines(group, carry):
            at = pl.multiple_of(group * GROUP, GROUP)
            for lane in range(0, step, 128):
                total = jnp.zeros((GROUP, 128), jnp.float32)
                place = index * step + lane
                for tap in range(KERNEL):
                    first = EDGE - half + tap
                    part = moved[first % 8, pl.ds(at + first // 8 * 8, GROUP), lane : lane + 128]
                    part = part * masks[tap, pl.ds(at, GROUP), :]
                    total = total + part * taps[tap : tap + 1, place : place + 128]
                act[pl.ds(at, GROUP), place : place + 128] = (total * jax.nn.sigmoid(total)).astype(
                    jnp.bfloat16
                )
            return carry

        lax.fori_loop(0, rows // GROUP, lines, 0)


def convolution(offsets, weight, context, low, own, up, gain, seg_wide, taps):
    rows, width = seg_wide.shape[0] // 3, own.shape[1]
    queries = rows + 2 * EDGE
    step = cut(width, 512)
    whole = pl.BlockSpec(memory_space=pltpu.VMEM)
    first = rows - KERNEL // 2
    seg_taps = jnp.stack([seg_wide[first + tap : first + tap + rows] for tap in range(KERNEL)], axis=1)
    return pl.pallas_call(
        functools.partial(convolution_kernel, len(weight)),
        out_shape=(
            jax.ShapeDtypeStruct((rows, width), jnp.bfloat16),
            jax.ShapeDtypeStruct((rows, width), jnp.float32),
        ),
        in_specs=[pl.BlockSpec(memory_space=pltpu.SMEM)]
        + [whole] * 8
        + [pl.BlockSpec(memory_space=pl.ANY)] * len(weight),
        out_specs=(whole, whole),
        scratch_shapes=[
            pltpu.VMEM((width, 3 * width), jnp.bfloat16),
            pltpu.VMEM((queries, width), jnp.float32),
            pltpu.VMEM((queries, width), jnp.bfloat16),
            pltpu.VMEM((queries + 8, step), jnp.float32),
            pltpu.VMEM((8, queries, step), jnp.float32),
            pltpu.VMEM((KERNEL, rows, 128), jnp.float32),
            pltpu.SemaphoreType.DMA((3 * width // step,)),
        ],
        compiler_params=pltpu.CompilerParams(vmem_limit_bytes=VMEM_BYTES),
        cost_estimate=pl.CostEstimate(
            flops=6 * width * width * queries + 3 * KERNEL * rows * width,
            bytes_accessed=6 * width * width + 8 * rows * width,
            transcendentals=2 * rows * width,
        ),
        name="convolution",
    )(
        offsets, context, low, own, up, gain, seg_wide[rows : 2 * rows][:, None], seg_taps, taps, *weight
    )


def mixing_kernel(pieces, offsets, act, resid, *rest):
    weight, (out, matrix, sems) = rest[:pieces], rest[pieces:]
    width = act.shape[1]
    step = cut(width, 512)
    spans = [pl.ds(at, step) for at in range(0, width, step)]
    for index, span in enumerate(spans):
        load_columns(offsets, weight, matrix, span, sems.at[index])
    for index, span in enumerate(spans):
        await_columns(matrix, span, sems.at[index])
        made = jnp.dot(act[...], matrix[:, span], preferred_element_type=jnp.float32)
        out[:, span] = (resid[:, span] + made).astype(jnp.bfloat16)


def mixing(offsets, weight, act, resid):
    rows, width = act.shape
    whole = pl.BlockSpec(memory_space=pltpu.VMEM)
    return pl.pallas_call(
        functools.partial(mixing_kernel, len(weight)),
        out_shape=jax.ShapeDtypeStruct((rows, width), jnp.bfloat16),
        in_specs=[pl.BlockSpec(memory_space=pltpu.SMEM)]
        + [whole] * 2
        + [pl.BlockSpec(memory_space=pl.ANY)] * len(weight),
        out_specs=whole,
        scratch_shapes=[
            pltpu.VMEM((width, width), jnp.bfloat16),
            pltpu.SemaphoreType.DMA((width // cut(width, 512),)),
        ],
        compiler_params=pltpu.CompilerParams(vmem_limit_bytes=VMEM_BYTES),
        cost_estimate=pl.CostEstimate(
            flops=2 * width * width * rows, bytes_accessed=2 * width * width + 8 * rows * width, transcendentals=0
        ),
        name="mixing",
    )(offsets, act, resid, *weight)


def on_device(
    layout,
    newcomer_groups,
    pending_inputs,
    speaker_clip_ids,
    selfattend_scaling,
    triple_projection_matrix,
    selfattend_final_matrix,
    depthwise_scaling,
    sigmoid_expand_matrix,
    filter_taps,
    combine_channel_matrix,
):
    core = lax.axis_index("section") % 2
    high = lax.axis_index("frame") // layout.half
    section = lax.axis_index("section") // 2 * 2 + high
    sections = layout.sections
    ticks = newcomer_groups.shape[0] + 1

    rows, width = pending_inputs.shape[1:]
    batches = speaker_clip_ids.shape[0]
    weights = Weights(layout)
    offsets = weights.offsets(combine_channel_matrix.shape[1])

    small = jnp.concatenate([selfattend_scaling, depthwise_scaling, filter_taps[0]], axis=0)
    small = jnp.where(core == high, small, send(small, layout.flipped(1, 0)))
    gain_a, gain_c, taps = small[0:1], small[1:2], small[2:]

    ids = (speaker_clip_ids + 1).astype(jnp.bfloat16)
    ids = jnp.pad(ids, ((0, -batches % 16), (0, width - rows)))
    own_1 = weights.to_half(behind(triple_projection_matrix[0], small))
    packed = jnp.concatenate([pending_inputs[0], ids], axis=0)
    packed = send(behind(packed, own_1), layout.to_workers())
    expand = jnp.concatenate([selfattend_final_matrix[0], sigmoid_expand_matrix[0]], axis=1)
    own_2 = weights.to_half(behind(expand, own_1))
    own_3 = weights.to_half(behind(combine_channel_matrix[0], own_2))
    sides_1 = weights.to_sides(own_1)
    sides_2 = weights.to_sides(behind(own_2, sides_1))
    packed_out = behind(packed, sides_1)
    packed = (send(packed_out, layout.shifted(1)), packed, send(packed_out, layout.shifted(-1)))
    diagonal_1 = weights.to_diagonal(*sides_1)
    qkv = weights.whole(own_1, sides_1, diagonal_1, packed, own_3)
    packed = behind(packed, own_3)

    ids = jnp.concatenate([part[rows : rows + batches, :rows] for part in packed], axis=1)
    ids = ids.astype(jnp.int32)
    low, present, up = packed

    made_all = []
    for tick in range(ticks):
        batch = sections - 1 - section + tick
        seg_wide = lax.dynamic_index_in_dim(ids, batch, 0, keepdims=False)
        context = attention(offsets, qkv, low, present, up, gain_a, seg_wide)
        if tick == 0:
            diagonal_2 = weights.to_diagonal(*behind(sides_2, context))
            sides_3 = weights.to_sides(behind(own_3, sides_2, context))
            out_expand = weights.whole(own_2, sides_2, diagonal_2)
            diagonal_3 = weights.to_diagonal(*behind(sides_3, diagonal_2))
            newcomers = behind(newcomer_groups, diagonal_2)
            newcomers = [send(newcomers[coming], layout.first()) for coming in range(ticks - 1)]
        act, resid = convolution(offsets, out_expand, context, low, present, up, gain_c, seg_wide, taps)
        if tick == 0:
            mix = weights.whole(own_3, sides_3, diagonal_3, act)
        made = mixing(offsets, mix, act, resid)
        made_all.append(send(made, layout.to_homes()))
        if tick + 1 < ticks:
            arrived = send(made, layout.relay())
            present = jnp.where(section == 0, newcomers[tick], arrived)
            low, up = send(present, layout.shifted(1)), send(present, layout.shifted(-1))
    return jnp.stack(made_all)[:, None]


def solution(mesh):
    layout = Layout(mesh.shape["section"], mesh.shape["frame"])
    in_specs = (
        P(None, "frame", None),
        P("section", "frame", None),
        P(None, "frame"),
        P("section", None),
        P("section", "frame", None),
        P("section", "frame", None),
        P("section", None),
        P("section", "frame", None),
        P("section", None, None),
        P("section", "frame", None),
    )
    out_specs = P(None, "section", "frame", None)

    def local(*args):
        return on_device(layout, *args)

    return jax.shard_map(
        local, mesh=mesh, in_specs=in_specs, out_specs=out_specs, check_vma=False
    )
```

```python
import functools

import jax
import jax.numpy as jnp
from jax import lax
from jax.experimental import pallas as pl
from jax.experimental.pallas import tpu as pltpu
from jax.sharding import PartitionSpec as P

HEADS = 24
KERNEL = 31
EPS = 1e-05
EDGE = 16
GROUP = 32
VMEM_BYTES = 56 * 1024 * 1024
TICK_VMEM_BYTES = 60 * 1024 * 1024
AXES = ("section", "frame")


class Layout:
    def __init__(self, sections, frames):
        self.sections, self.frames, self.half = sections, frames, frames // 2
        self.gray = [r ^ (r >> 1) for r in range(self.half)]
        if sorted(self.gray) != list(range(self.half)):
            self.gray = list(range(self.half))

    def flat(self, section, frame):
        return section * self.frames + frame

    def worker(self, section, block):
        pair, high = divmod(section, 2)
        return self.flat(2 * pair + block % 2, high * self.half + self.gray.index(block // 2))

    def each(self):
        return [(s, b) for s in range(self.sections) for b in range(self.frames)]

    def to_workers(self, step=0):
        return [
            (self.flat(s, b + step), self.worker(s, b))
            for s, b in self.each()
            if 0 <= b + step < self.frames
        ]

    def to_homes(self):
        return [(there, here) for here, there in self.to_workers()]

    def shifted(self, step):
        return [
            (self.worker(s, b), self.worker(s, b + step))
            for s, b in self.each()
            if 0 <= b + step < self.frames
        ]

    def relay(self):
        return [
            (self.worker(s, b), self.worker(s + 1, b)) for s, b in self.each() if s + 1 < self.sections
        ]

    def first(self):
        return [(self.flat(0, b), self.worker(0, b)) for b in range(self.frames)]

    def rows_to_half(self):
        moves = []
        for s, f in self.each():
            (pair, high), (core, rest) = divmod(s, 2), divmod(f, self.half)
            if core != high:
                moves.append((self.flat(s, f), self.flat(2 * pair + core, high * self.half + rest)))
        return moves

    def flipped(self, section_bit, frame_bits):
        return [(self.flat(s, f), self.flat(s ^ section_bit, f ^ frame_bits)) for s, f in self.each()]

    def diagonal(self):
        return [
            (self.flat(s, f), self.flat(s, f ^ (1 if s % 2 == f // self.half else 2)))
            for s, f in self.each()
        ]

    def groups(self):
        return [
            [self.flat(2 * k + c, h * self.half + r) for c in range(2) for r in range(self.half)]
            for k in range(self.sections // 2)
            for h in range(2)
        ]


def send(value, moves):
    return lax.ppermute(value, AXES, moves)


def behind(value, *earlier):
    return lax.optimization_barrier((value, earlier))[0]


class Weights:
    def __init__(self, layout):
        self.layout = layout
        self.core = lax.axis_index("section") % 2
        self.rest = lax.axis_index("frame") % layout.half
        self.at_home = self.core == lax.axis_index("frame") // layout.half
        self.tree = layout.half == 4

    def to_half(self, chunk):
        return jnp.where(self.at_home, chunk, send(chunk, self.layout.rows_to_half()))

    def to_sides(self, own):
        if not self.tree:
            return own, own
        return send(own, self.layout.flipped(0, 1)), send(own, self.layout.flipped(0, 2))

    def to_diagonal(self, along_x, along_z):
        if not self.tree:
            return along_x, along_z
        half = along_x.shape[1] // 2
        low = send(along_z[:, :half], self.layout.flipped(0, 1))
        high = jnp.where(self.at_home, along_z[:, half:], along_x[:, half:])
        return low, send(high, self.layout.diagonal())

    def offsets(self, rows):
        if not self.tree:
            return jnp.zeros((1,), jnp.int32)
        near = self.core * 4 + (jnp.arange(4) ^ self.rest)
        return jnp.concatenate([near, near ^ 4]).astype(jnp.int32) * rows

    def whole(self, own, sides, diagonal, *earlier):
        if not self.tree:
            whole = lax.all_gather(
                own, AXES, axis=0, tiled=True, axis_index_groups=self.layout.groups()
            )
            return (whole[None],)
        own, sides, diagonal = behind((own, sides, diagonal), *earlier)
        near = jnp.stack([own, *sides, jnp.concatenate(diagonal, axis=1)])
        return near, send(near, self.layout.flipped(1, 0))


def cut(total, most):
    return max(w for w in range(128, most + 1, 128) if total % w == 0)


def load_columns(offsets, pieces, target, columns, sem):
    place = 0
    for piece in pieces:
        count, height = piece.shape[:2]
        for index in range(count):
            row = pl.multiple_of(offsets[place], 16)
            place += 1
            pltpu.make_async_copy(
                piece.at[index, :, columns], target.at[pl.ds(row, height), columns], sem
            ).start()


def await_columns(target, columns, sem):
    pltpu.make_async_copy(target.at[:, columns], target.at[:, columns], sem).wait()


def normalised(lines, gain):
    mean = jnp.mean(lines, axis=-1, keepdims=True)
    centred = lines - mean
    spread = jnp.mean(centred * centred, axis=-1, keepdims=True)
    return (centred * lax.rsqrt(spread + EPS) * gain).astype(jnp.bfloat16)


def attention_kernel(pieces, offsets, low, own, up, gain, seg_rows, seg_keys, *rest):
    attend(offsets, rest[:pieces], low, own, up, gain, seg_rows, seg_keys, *rest[pieces:])


def attend(
    offsets, weight, low, own, up, gain, seg_rows, seg_keys,
    context, matrix, normed, query, keys, values, bias, sems, asked_all=None, projected=None,
):
    queries, width = context.shape
    rows = queries - 2 * EDGE
    wide, start = 3 * rows, rows - EDGE
    step = cut(width, 768)
    spans = [pl.ds(at, step) for at in range(0, 3 * width, step)]
    for index, span in enumerate(spans):
        load_columns(offsets, weight, matrix, span, sems.at[index])
    if asked_all is not None:
        asked_all()
    for index, block in enumerate((low, own, up)):
        normed[pl.ds(index * rows, rows), :] = normalised(
            block[pl.ds(0, rows), :].astype(jnp.float32), gain[...]
        )
    tile, window = queries // 2, 2 * rows + 128
    firsts = (0, wide - window)
    for part in range(2):
        same = seg_rows[pl.ds(part * tile, tile), :] == seg_keys[:, pl.ds(firsts[part], window)]
        sheet = jnp.where(same, 0.0, -1e30)
        bias[part, pl.ds(0, tile), :] = sheet
        bias[part, pl.ds(tile, tile), :] = sheet
    per = width // step
    for index, span in enumerate(spans):
        await_columns(matrix, span, sems.at[index])
        kind, at = divmod(index, per)
        place = pl.ds(at * step, step)
        if kind == 0:
            made = jnp.dot(
                normed[pl.ds(start, queries), :], matrix[:, span], preferred_element_type=jnp.float32
            )
            query[:, place] = (made * (width // HEADS) ** (-0.5)).astype(jnp.bfloat16)
        else:
            made = jnp.dot(normed[...], matrix[:, span], preferred_element_type=jnp.float32)
            (keys if kind == 1 else values)[:, place] = made.astype(jnp.bfloat16)

    if projected is not None:
        projected()
    head = width // HEADS
    together = 128 // head
    lanes = lax.broadcasted_iota(jnp.int32, (tile, 128), 1) // head
    ones = jnp.ones((window, 128), jnp.bfloat16)

    def heads(index, carry):
        place = pl.ds(pl.multiple_of(index * 128, 128), 128)
        for part in range(2):
            asked = query[pl.ds(part * tile, tile), place]
            stacked = jnp.concatenate(
                [jnp.where(lanes == one, asked, jnp.zeros_like(asked)) for one in range(together)], axis=0
            )
            seen = pl.ds(firsts[part], window)
            scores = lax.dot_general(
                stacked, keys[seen, place], (((1,), (1,)), ((), ())), preferred_element_type=jnp.float32
            )
            scores = scores + bias[part]
            expd = jnp.exp(scores - jnp.max(scores, axis=-1, keepdims=True))
            shown = jnp.concatenate([values[seen, place], ones], axis=1)
            mixed = jnp.dot(expd.astype(jnp.bfloat16), shown, preferred_element_type=jnp.float32)
            mixed = mixed[:, :128] / mixed[:, 128:]
            result = mixed[:tile]
            for one in range(1, together):
                result = jnp.where(lanes == one, mixed[one * tile : (one + 1) * tile], result)
            context[pl.ds(part * tile, tile), place] = result.astype(jnp.bfloat16)
        return carry

    lax.fori_loop(0, width // 128, heads, 0, unroll=2)


def attention(offsets, weight, low, own, up, gain, seg_wide):
    rows, width = seg_wide.shape[0] // 3, own.shape[1]
    wide, queries = 3 * rows, rows + 2 * EDGE
    spans = 3 * width // cut(width, 768)
    whole = pl.BlockSpec(memory_space=pltpu.VMEM)
    seg_rows = seg_wide[rows - EDGE : 2 * rows + EDGE][:, None]
    return pl.pallas_call(
        functools.partial(attention_kernel, len(weight)),
        out_shape=jax.ShapeDtypeStruct((queries, width), jnp.bfloat16),
        in_specs=[pl.BlockSpec(memory_space=pltpu.SMEM)]
        + [whole] * 6
        + [pl.BlockSpec(memory_space=pl.ANY)] * len(weight),
        out_specs=whole,
        scratch_shapes=[
            pltpu.VMEM((width, 3 * width), jnp.bfloat16),
            pltpu.VMEM((wide, width), jnp.bfloat16),
            pltpu.VMEM((queries, width), jnp.bfloat16),
            pltpu.VMEM((wide, width), jnp.bfloat16),
            pltpu.VMEM((wide, width), jnp.bfloat16),
            pltpu.VMEM((2, queries, 2 * rows + 128), jnp.float32),
            pltpu.SemaphoreType.DMA((spans,)),
        ],
        compiler_params=pltpu.CompilerParams(vmem_limit_bytes=VMEM_BYTES),
        cost_estimate=pl.CostEstimate(
            flops=2 * width * width * (queries + 2 * wide) + 4 * queries * wide * width,
            bytes_accessed=6 * width * width + 8 * rows * width,
            transcendentals=HEADS * queries * wide,
        ),
        name="attention",
    )(offsets, low, own, up, gain, seg_rows, seg_wide[None, :], *weight)


def convolution_kernel(
    pieces, offsets, context, low, own, up, gain, seg_rows, masks_seg, taps, *rest
):
    weight, (act, resid_out, matrix, resid, *scratch) = rest[:pieces], rest[pieces:]
    ask_for_expansion(offsets, weight, matrix, scratch[-1])
    convolve(context, low, own, up, gain, seg_rows, masks_seg, taps, act, matrix, resid, *scratch)
    resid_out[...] = resid[pl.ds(EDGE, act.shape[0]), :]


def expansion_spans(width):
    step = cut(width, 512)
    outs, values, gates = (
        [pl.ds(part * width + at, step) for at in range(0, width, step)] for part in range(3)
    )
    return outs, values, gates, outs + [span for both in zip(values, gates) for span in both]


def ask_for_expansion(offsets, weight, matrix, sems):
    for index, span in enumerate(expansion_spans(matrix.shape[0])[3]):
        load_columns(offsets, weight, matrix, span, sems.at[index])


def convolve(
    context, low, own, up, gain, seg_rows, masks_seg, taps, act, matrix, resid, conv_in, gated, moved, masks, sems
):
    rows, width = act.shape
    queries = rows + 2 * EDGE
    step = cut(width, 512)
    count = width // step
    outs, values, gates, _ = expansion_spans(width)
    half = KERNEL // 2
    for tap in range(KERNEL):
        same = masks_seg[:, tap : tap + 1] == seg_rows[...]
        masks[tap] = jnp.broadcast_to(jnp.where(same, 1.0, 0.0), (rows, 128))
    for index, span in enumerate(outs):
        await_columns(matrix, span, sems.at[index])
        added = jnp.dot(context[...], matrix[:, span], preferred_element_type=jnp.float32)
        resid[pl.ds(0, EDGE), span] = added[:EDGE] + low[pl.ds(rows - EDGE, EDGE), span].astype(jnp.float32)
        resid[pl.ds(EDGE, rows), span] = added[EDGE : EDGE + rows] + own[pl.ds(0, rows), span].astype(jnp.float32)
        resid[pl.ds(EDGE + rows, EDGE), span] = added[EDGE + rows :] + up[pl.ds(0, EDGE), span].astype(
            jnp.float32
        )
    conv_in[...] = normalised(resid[...], gain[...])
    for index in range(count):
        await_columns(matrix, values[index], sems.at[count + 2 * index])
        await_columns(matrix, gates[index], sems.at[count + 2 * index + 1])
        value = jnp.dot(conv_in[...], matrix[:, values[index]], preferred_element_type=jnp.float32)
        gate = jnp.dot(conv_in[...], matrix[:, gates[index]], preferred_element_type=jnp.float32)
        glu = (value * jax.nn.sigmoid(gate)).astype(jnp.bfloat16).astype(jnp.float32)
        gated[pl.ds(0, queries), :] = glu
        for shift in range(8):
            moved[shift] = gated[pl.ds(shift, queries), :]

        def lines(group, carry):
            at = pl.multiple_of(group * GROUP, GROUP)
            lanes = range(0, step, 128)
            totals = [jnp.zeros((GROUP, 128), jnp.float32) for _ in lanes]
            for tap in range(KERNEL):
                first = EDGE - half + tap
                mask = masks[tap, pl.ds(at, GROUP), :]
                for number, lane in enumerate(lanes):
                    place = index * step + lane
                    part = moved[first % 8, pl.ds(at + first // 8 * 8, GROUP), lane : lane + 128]
                    totals[number] += part * mask * taps[tap : tap + 1, place : place + 128]
            for total, lane in zip(totals, lanes):
                place = index * step + lane
                act[pl.ds(at, GROUP), place : place + 128] = (total * jax.nn.sigmoid(total)).astype(
                    jnp.bfloat16
                )
            return carry

        lax.fori_loop(0, rows // GROUP, lines, 0)


def convolution(offsets, weight, context, low, own, up, gain, seg_wide, taps):
    rows, width = seg_wide.shape[0] // 3, own.shape[1]
    queries = rows + 2 * EDGE
    step = cut(width, 512)
    whole = pl.BlockSpec(memory_space=pltpu.VMEM)
    first = rows - KERNEL // 2
    seg_taps = jnp.stack([seg_wide[first + tap : first + tap + rows] for tap in range(KERNEL)], axis=1)
    return pl.pallas_call(
        functools.partial(convolution_kernel, len(weight)),
        out_shape=(
            jax.ShapeDtypeStruct((rows, width), jnp.bfloat16),
            jax.ShapeDtypeStruct((rows, width), jnp.float32),
        ),
        in_specs=[pl.BlockSpec(memory_space=pltpu.SMEM)]
        + [whole] * 8
        + [pl.BlockSpec(memory_space=pl.ANY)] * len(weight),
        out_specs=(whole, whole),
        scratch_shapes=[
            pltpu.VMEM((width, 3 * width), jnp.bfloat16),
            pltpu.VMEM((queries, width), jnp.float32),
            pltpu.VMEM((queries, width), jnp.bfloat16),
            pltpu.VMEM((queries + 8, step), jnp.float32),
            pltpu.VMEM((8, queries, step), jnp.float32),
            pltpu.VMEM((KERNEL, rows, 128), jnp.float32),
            pltpu.SemaphoreType.DMA((3 * width // step,)),
        ],
        compiler_params=pltpu.CompilerParams(vmem_limit_bytes=VMEM_BYTES),
        cost_estimate=pl.CostEstimate(
            flops=6 * width * width * queries + 3 * KERNEL * rows * width,
            bytes_accessed=6 * width * width + 8 * rows * width,
            transcendentals=2 * rows * width,
        ),
        name="convolution",
    )(
        offsets, context, low, own, up, gain, seg_wide[rows : 2 * rows][:, None], seg_taps, taps, *weight
    )


def mixing_kernel(pieces, offsets, act, resid, *rest):
    weight, (out, matrix, sems) = rest[:pieces], rest[pieces:]
    width = act.shape[1]
    step = cut(width, 512)
    spans = [pl.ds(at, step) for at in range(0, width, step)]
    for index, span in enumerate(spans):
        load_columns(offsets, weight, matrix, span, sems.at[index])
    for index, span in enumerate(spans):
        await_columns(matrix, span, sems.at[index])
        made = jnp.dot(act[...], matrix[:, span], preferred_element_type=jnp.float32)
        out[:, span] = (resid[:, span] + made).astype(jnp.bfloat16)


def mixing(offsets, weight, act, resid):
    rows, width = act.shape
    whole = pl.BlockSpec(memory_space=pltpu.VMEM)
    return pl.pallas_call(
        functools.partial(mixing_kernel, len(weight)),
        out_shape=jax.ShapeDtypeStruct((rows, width), jnp.bfloat16),
        in_specs=[pl.BlockSpec(memory_space=pltpu.SMEM)]
        + [whole] * 2
        + [pl.BlockSpec(memory_space=pl.ANY)] * len(weight),
        out_specs=whole,
        scratch_shapes=[
            pltpu.VMEM((width, width), jnp.bfloat16),
            pltpu.SemaphoreType.DMA((width // cut(width, 512),)),
        ],
        compiler_params=pltpu.CompilerParams(vmem_limit_bytes=VMEM_BYTES),
        cost_estimate=pl.CostEstimate(
            flops=2 * width * width * rows, bytes_accessed=2 * width * width + 8 * rows * width, transcendentals=0
        ),
        name="mixing",
    )(offsets, act, resid, *weight)


def tick_kernel(counts, offsets, low, own, up, gain_a, gain_c, seg_queries, seg_keys, seg_rows, masks_seg, taps, *rest):
    first, second, third = counts
    qkv, rest = rest[:first], rest[first:]
    expand, rest = rest[:second], rest[second:]
    mix, rest = rest[:third], rest[third:]
    out, context, matrix, normed, query, keys, values, bias, sems, act, expansion, resid, *scratch, mix_sems = rest
    rows, width = out.shape
    step = cut(width, 512)
    spans = [pl.ds(at, step) for at in range(0, width, step)]

    def ask_for_mix():
        for index, span in enumerate(spans):
            load_columns(offsets, mix, matrix, span, mix_sems.at[index])

    attend(
        offsets, qkv, low, own, up, gain_a, seg_queries, seg_keys,
        context, matrix, normed, query, keys, values, bias, sems,
        lambda: ask_for_expansion(offsets, expand, expansion, scratch[-1]), ask_for_mix,
    )
    convolve(context, low, own, up, gain_c, seg_rows, masks_seg, taps, act, expansion, resid, *scratch)
    for index, span in enumerate(spans):
        await_columns(matrix, span, mix_sems.at[index])
        made = jnp.dot(act[...], matrix[:, span], preferred_element_type=jnp.float32)
        out[:, span] = (resid[pl.ds(EDGE, rows), span] + made).astype(jnp.bfloat16)


def whole_tick(offsets, qkv, expand, mix, low, own, up, gain_a, gain_c, seg_wide, taps):
    rows, width = seg_wide.shape[0] // 3, own.shape[1]
    wide, queries, step = 3 * rows, rows + 2 * EDGE, cut(width, 512)
    whole = pl.BlockSpec(memory_space=pltpu.VMEM)
    first = rows - KERNEL // 2
    seg_taps = jnp.stack([seg_wide[first + tap : first + tap + rows] for tap in range(KERNEL)], axis=1)
    pieces = (*qkv, *expand, *mix)
    return pl.pallas_call(
        functools.partial(tick_kernel, (len(qkv), len(expand), len(mix))),
        out_shape=jax.ShapeDtypeStruct((rows, width), jnp.bfloat16),
        in_specs=[pl.BlockSpec(memory_space=pltpu.SMEM)]
        + [whole] * 10
        + [pl.BlockSpec(memory_space=pl.ANY)] * len(pieces),
        out_specs=whole,
        scratch_shapes=[
            pltpu.VMEM((queries, width), jnp.bfloat16),
            pltpu.VMEM((width, 3 * width), jnp.bfloat16),
            pltpu.VMEM((wide, width), jnp.bfloat16),
            pltpu.VMEM((queries, width), jnp.bfloat16),
            pltpu.VMEM((wide, width), jnp.bfloat16),
            pltpu.VMEM((wide, width), jnp.bfloat16),
            pltpu.VMEM((2, queries, 2 * rows + 128), jnp.float32),
            pltpu.SemaphoreType.DMA((3 * width // cut(width, 768),)),
            pltpu.VMEM((rows, width), jnp.bfloat16),
            pltpu.VMEM((width, 3 * width), jnp.bfloat16),
            pltpu.VMEM((queries, width), jnp.float32),
            pltpu.VMEM((queries, width), jnp.bfloat16),
            pltpu.VMEM((queries + 8, step), jnp.float32),
            pltpu.VMEM((8, queries, step), jnp.float32),
            pltpu.VMEM((KERNEL, rows, 128), jnp.float32),
            pltpu.SemaphoreType.DMA((3 * width // step,)),
            pltpu.SemaphoreType.DMA((width // step,)),
        ],
        compiler_params=pltpu.CompilerParams(vmem_limit_bytes=TICK_VMEM_BYTES),
        cost_estimate=pl.CostEstimate(
            flops=2 * width * width * (5 * queries + 2 * wide), bytes_accessed=14 * width * width, transcendentals=0
        ),
        name="tick",
    )(
        offsets, low, own, up, gain_a, gain_c,
        seg_wide[rows - EDGE : 2 * rows + EDGE][:, None], seg_wide[None, :],
        seg_wide[rows : 2 * rows][:, None], seg_taps, taps, *pieces,
    )


def on_device(
    layout,
    newcomer_groups,
    pending_inputs,
    speaker_clip_ids,
    selfattend_scaling,
    triple_projection_matrix,
    selfattend_final_matrix,
    depthwise_scaling,
    sigmoid_expand_matrix,
    filter_taps,
    combine_channel_matrix,
):
    core = lax.axis_index("section") % 2
    high = lax.axis_index("frame") // layout.half
    section = lax.axis_index("section") // 2 * 2 + high
    sections = layout.sections
    ticks = newcomer_groups.shape[0] + 1

    rows, width = pending_inputs.shape[1:]
    batches = speaker_clip_ids.shape[0]
    weights = Weights(layout)
    offsets = weights.offsets(combine_channel_matrix.shape[1])

    small = jnp.concatenate([selfattend_scaling, depthwise_scaling, filter_taps[0]], axis=0)
    small = jnp.where(core == high, small, send(small, layout.flipped(1, 0)))
    gain_a, gain_c, taps = small[0:1], small[1:2], small[2:]

    ids = (speaker_clip_ids + 1).astype(jnp.bfloat16)
    ids = jnp.pad(ids, ((0, -batches % 16), (0, width - rows)))
    own_1 = weights.to_half(behind(triple_projection_matrix[0], small))
    packed = jnp.concatenate([pending_inputs[0], ids], axis=0)
    packed = send(behind(packed, own_1), layout.to_workers())
    expand = jnp.concatenate([selfattend_final_matrix[0], sigmoid_expand_matrix[0]], axis=1)
    own_2 = weights.to_half(behind(expand, own_1))
    own_3 = weights.to_half(behind(combine_channel_matrix[0], own_2))
    sides_1 = weights.to_sides(own_1)
    sides_2 = weights.to_sides(behind(own_2, sides_1))
    packed_out = behind(packed, sides_1)
    packed = (send(packed_out, layout.shifted(1)), packed, send(packed_out, layout.shifted(-1)))
    diagonal_1 = weights.to_diagonal(*sides_1)
    qkv = weights.whole(own_1, sides_1, diagonal_1, packed, own_3)
    packed = behind(packed, own_3)

    ids = jnp.concatenate([part[rows : rows + batches, :rows] for part in packed], axis=1)
    ids = ids.astype(jnp.int32)
    low, present, up = packed

    made_all = []
    for tick in range(ticks):
        batch = sections - 1 - section + tick
        seg_wide = lax.dynamic_index_in_dim(ids, batch, 0, keepdims=False)
        if tick > 0:
            made = whole_tick(offsets, qkv, out_expand, mix, low, present, up, gain_a, gain_c, seg_wide, taps)
        else:
            context = attention(offsets, qkv, low, present, up, gain_a, seg_wide)
            diagonal_2 = weights.to_diagonal(*behind(sides_2, context))
            sides_3 = weights.to_sides(behind(own_3, sides_2, context))
            out_expand = weights.whole(own_2, sides_2, diagonal_2)
            diagonal_3 = weights.to_diagonal(*behind(sides_3, diagonal_2))
            newcomers = behind(newcomer_groups, diagonal_2)
            newcomers = [send(newcomers[coming], layout.first()) for coming in range(ticks - 1)]
            act, resid = convolution(offsets, out_expand, context, low, present, up, gain_c, seg_wide, taps)
            mix = weights.whole(own_3, sides_3, diagonal_3, act)
            made = mixing(offsets, mix, act, resid)
        made_all.append(send(made, layout.to_homes()))
        if tick + 1 < ticks:
            arrived = send(made, layout.relay())
            present = jnp.where(section == 0, newcomers[tick], arrived)
            low, up = send(present, layout.shifted(1)), send(present, layout.shifted(-1))
    return jnp.stack(made_all)[:, None]


def solution(mesh):
    layout = Layout(mesh.shape["section"], mesh.shape["frame"])
    in_specs = (
        P(None, "frame", None),
        P("section", "frame", None),
        P(None, "frame"),
        P("section", None),
        P("section", "frame", None),
        P("section", "frame", None),
        P("section", None),
        P("section", "frame", None),
        P("section", None, None),
        P("section", "frame", None),
    )
    out_specs = P(None, "section", "frame", None)

    def local(*args):
        return on_device(layout, *args)

    return jax.shard_map(
        local, mesh=mesh, in_specs=in_specs, out_specs=out_specs, check_vma=False
    )
```

```python
import functools

import jax
import jax.numpy as jnp
from jax import lax
from jax.experimental import pallas as pl
from jax.experimental.pallas import tpu as pltpu
from jax.sharding import PartitionSpec as P

HEADS = 24
KERNEL = 31
EPS = 1e-05
EDGE = 16
GROUP = 32
VMEM_BYTES = 56 * 1024 * 1024
TICK_VMEM_BYTES = 60 * 1024 * 1024
AXES = ("section", "frame")


class Layout:
    def __init__(self, sections, frames):
        self.sections, self.frames, self.half = sections, frames, frames // 2
        self.gray = [r ^ (r >> 1) for r in range(self.half)]
        if sorted(self.gray) != list(range(self.half)):
            self.gray = list(range(self.half))

    def flat(self, section, frame):
        return section * self.frames + frame

    def worker(self, section, block):
        pair, high = divmod(section, 2)
        return self.flat(2 * pair + block % 2, high * self.half + self.gray.index(block // 2))

    def each(self):
        return [(s, b) for s in range(self.sections) for b in range(self.frames)]

    def to_workers(self, step=0):
        return [
            (self.flat(s, b + step), self.worker(s, b))
            for s, b in self.each()
            if 0 <= b + step < self.frames
        ]

    def to_homes(self):
        return [(there, here) for here, there in self.to_workers()]

    def shifted(self, step):
        return [
            (self.worker(s, b), self.worker(s, b + step))
            for s, b in self.each()
            if 0 <= b + step < self.frames
        ]

    def relay(self):
        return [
            (self.worker(s, b), self.worker(s + 1, b)) for s, b in self.each() if s + 1 < self.sections
        ]

    def first(self):
        return [(self.flat(0, b), self.worker(0, b)) for b in range(self.frames)]

    def rows_to_half(self):
        moves = []
        for s, f in self.each():
            (pair, high), (core, rest) = divmod(s, 2), divmod(f, self.half)
            if core != high:
                moves.append((self.flat(s, f), self.flat(2 * pair + core, high * self.half + rest)))
        return moves

    def flipped(self, section_bit, frame_bits):
        return [(self.flat(s, f), self.flat(s ^ section_bit, f ^ frame_bits)) for s, f in self.each()]

    def diagonal(self):
        return [
            (self.flat(s, f), self.flat(s, f ^ (1 if s % 2 == f // self.half else 2)))
            for s, f in self.each()
        ]

    def groups(self):
        return [
            [self.flat(2 * k + c, h * self.half + r) for c in range(2) for r in range(self.half)]
            for k in range(self.sections // 2)
            for h in range(2)
        ]


def send(value, moves):
    return lax.ppermute(value, AXES, moves)


def behind(value, *earlier):
    return lax.optimization_barrier((value, earlier))[0]


class Weights:
    def __init__(self, layout):
        self.layout = layout
        self.core = lax.axis_index("section") % 2
        self.rest = lax.axis_index("frame") % layout.half
        self.at_home = self.core == lax.axis_index("frame") // layout.half
        self.tree = layout.half == 4

    def to_half(self, chunk):
        return jnp.where(self.at_home, chunk, send(chunk, self.layout.rows_to_half()))

    def to_sides(self, own):
        if not self.tree:
            return own, own
        return send(own, self.layout.flipped(0, 1)), send(own, self.layout.flipped(0, 2))

    def to_diagonal(self, along_x, along_z, even):
        if not self.tree:
            return along_x, along_z
        half = along_x.shape[1] // 2
        low = send(along_z[:, :half], self.layout.flipped(0, 1))
        if even:
            return low, send(along_x[:, half:], self.layout.flipped(0, 2))
        high = jnp.where(self.at_home, along_z[:, half:], along_x[:, half:])
        return low, send(high, self.layout.diagonal())

    def offsets(self, rows):
        if not self.tree:
            return jnp.zeros((1,), jnp.int32)
        near = self.core * 4 + (jnp.arange(4) ^ self.rest)
        return jnp.concatenate([near, near ^ 4]).astype(jnp.int32) * rows

    def whole(self, own, sides, diagonal, *earlier):
        if not self.tree:
            whole = lax.all_gather(
                own, AXES, axis=0, tiled=True, axis_index_groups=self.layout.groups()
            )
            return (whole[None],)
        own, sides, diagonal = behind((own, sides, diagonal), *earlier)
        near = jnp.stack([own, *sides, jnp.concatenate(diagonal, axis=1)])
        return near, send(near, self.layout.flipped(1, 0))

    def whole_by_parts(self, own, sides, diagonal, *earlier):
        if not self.tree:
            return self.whole(own, sides, diagonal)
        own, sides = behind((own, sides), *earlier)
        near = jnp.stack([own, *sides])
        far = send(near, self.layout.flipped(1, 0))
        last = jnp.concatenate(diagonal, axis=1)[None]
        return near, last, far, send(last, self.layout.flipped(1, 0))


def cut(total, most):
    return max(w for w in range(128, most + 1, 128) if total % w == 0)


def load_columns(offsets, pieces, target, columns, sem):
    place = 0
    for piece in pieces:
        count, height = piece.shape[:2]
        for index in range(count):
            row = pl.multiple_of(offsets[place], 16)
            place += 1
            pltpu.make_async_copy(
                piece.at[index, :, columns], target.at[pl.ds(row, height), columns], sem
            ).start()


def await_columns(target, columns, sem):
    pltpu.make_async_copy(target.at[:, columns], target.at[:, columns], sem).wait()


def normalised(lines, gain):
    mean = jnp.mean(lines, axis=-1, keepdims=True)
    centred = lines - mean
    spread = jnp.mean(centred * centred, axis=-1, keepdims=True)
    return (centred * lax.rsqrt(spread + EPS) * gain).astype(jnp.bfloat16)


def attention_kernel(pieces, offsets, low, own, up, gain, seg_rows, seg_keys, *rest):
    attend(offsets, rest[:pieces], low, own, up, gain, seg_rows, seg_keys, *rest[pieces:])


def attend(
    offsets, weight, low, own, up, gain, seg_rows, seg_keys,
    context, matrix, normed, query, keys, values, bias, sems, asked_all=None, projected=None,
):
    queries, width = context.shape
    rows = queries - 2 * EDGE
    wide, start = 3 * rows, rows - EDGE
    step = cut(width, 768)
    spans = [pl.ds(at, step) for at in range(0, 3 * width, step)]
    for index, span in enumerate(spans):
        load_columns(offsets, weight, matrix, span, sems.at[index])
    if asked_all is not None:
        asked_all()
    for index, block in enumerate((low, own, up)):
        normed[pl.ds(index * rows, rows), :] = normalised(
            block[pl.ds(0, rows), :].astype(jnp.float32), gain[...]
        )
    tile, window = queries // 2, 2 * rows + 128
    firsts = (0, wide - window)
    for part in range(2):
        same = seg_rows[pl.ds(part * tile, tile), :] == seg_keys[:, pl.ds(firsts[part], window)]
        sheet = jnp.where(same, 0.0, -1e30)
        bias[part, pl.ds(0, tile), :] = sheet
        bias[part, pl.ds(tile, tile), :] = sheet
    per = width // step
    for index, span in enumerate(spans):
        await_columns(matrix, span, sems.at[index])
        kind, at = divmod(index, per)
        place = pl.ds(at * step, step)
        if kind == 0:
            made = jnp.dot(
                normed[pl.ds(start, queries), :], matrix[:, span], preferred_element_type=jnp.float32
            )
            query[:, place] = (made * (width // HEADS) ** (-0.5)).astype(jnp.bfloat16)
        else:
            made = jnp.dot(normed[...], matrix[:, span], preferred_element_type=jnp.float32)
            (keys if kind == 1 else values)[:, place] = made.astype(jnp.bfloat16)

    if projected is not None:
        projected()
    head = width // HEADS
    together = 128 // head
    lanes = lax.broadcasted_iota(jnp.int32, (tile, 128), 1) // head
    ones = jnp.ones((window, 128), jnp.bfloat16)

    def heads(index, carry):
        place = pl.ds(pl.multiple_of(index * 128, 128), 128)
        for part in range(2):
            asked = query[pl.ds(part * tile, tile), place]
            stacked = jnp.concatenate(
                [jnp.where(lanes == one, asked, jnp.zeros_like(asked)) for one in range(together)], axis=0
            )
            seen = pl.ds(firsts[part], window)
            scores = lax.dot_general(
                stacked, keys[seen, place], (((1,), (1,)), ((), ())), preferred_element_type=jnp.float32
            )
            scores = scores + bias[part]
            expd = jnp.exp(scores - jnp.max(scores, axis=-1, keepdims=True))
            shown = jnp.concatenate([values[seen, place], ones], axis=1)
            mixed = jnp.dot(expd.astype(jnp.bfloat16), shown, preferred_element_type=jnp.float32)
            mixed = mixed[:, :128] / mixed[:, 128:]
            result = mixed[:tile]
            for one in range(1, together):
                result = jnp.where(lanes == one, mixed[one * tile : (one + 1) * tile], result)
            context[pl.ds(part * tile, tile), place] = result.astype(jnp.bfloat16)
        return carry

    lax.fori_loop(0, width // 128, heads, 0, unroll=2)


def attention(offsets, weight, low, own, up, gain, seg_wide):
    rows, width = seg_wide.shape[0] // 3, own.shape[1]
    wide, queries = 3 * rows, rows + 2 * EDGE
    spans = 3 * width // cut(width, 768)
    whole = pl.BlockSpec(memory_space=pltpu.VMEM)
    seg_rows = seg_wide[rows - EDGE : 2 * rows + EDGE][:, None]
    return pl.pallas_call(
        functools.partial(attention_kernel, len(weight)),
        out_shape=jax.ShapeDtypeStruct((queries, width), jnp.bfloat16),
        in_specs=[pl.BlockSpec(memory_space=pltpu.SMEM)]
        + [whole] * 6
        + [pl.BlockSpec(memory_space=pl.ANY)] * len(weight),
        out_specs=whole,
        scratch_shapes=[
            pltpu.VMEM((width, 3 * width), jnp.bfloat16),
            pltpu.VMEM((wide, width), jnp.bfloat16),
            pltpu.VMEM((queries, width), jnp.bfloat16),
            pltpu.VMEM((wide, width), jnp.bfloat16),
            pltpu.VMEM((wide, width), jnp.bfloat16),
            pltpu.VMEM((2, queries, 2 * rows + 128), jnp.float32),
            pltpu.SemaphoreType.DMA((spans,)),
        ],
        compiler_params=pltpu.CompilerParams(vmem_limit_bytes=VMEM_BYTES),
        cost_estimate=pl.CostEstimate(
            flops=2 * width * width * (queries + 2 * wide) + 4 * queries * wide * width,
            bytes_accessed=6 * width * width + 8 * rows * width,
            transcendentals=HEADS * queries * wide,
        ),
        name="attention",
    )(offsets, low, own, up, gain, seg_rows, seg_wide[None, :], *weight)


def convolution_kernel(
    pieces, offsets, context, low, own, up, gain, seg_rows, masks_seg, taps, *rest
):
    weight, (act, resid_out, matrix, resid, *scratch) = rest[:pieces], rest[pieces:]
    ask_for_expansion(offsets, weight, matrix, scratch[-1])
    convolve(context, low, own, up, gain, seg_rows, masks_seg, taps, act, matrix, resid, *scratch)
    resid_out[...] = resid[pl.ds(EDGE, act.shape[0]), :]


def expansion_spans(width):
    step = cut(width, 512)
    outs, values, gates = (
        [pl.ds(part * width + at, step) for at in range(0, width, step)] for part in range(3)
    )
    return outs, values, gates, outs + [span for both in zip(values, gates) for span in both]


def ask_for_expansion(offsets, weight, matrix, sems):
    for index, span in enumerate(expansion_spans(matrix.shape[0])[3]):
        load_columns(offsets, weight, matrix, span, sems.at[index])


def convolve(
    context, low, own, up, gain, seg_rows, masks_seg, taps, act, matrix, resid, conv_in, gated, moved, masks, sems
):
    rows, width = act.shape
    queries = rows + 2 * EDGE
    step = cut(width, 512)
    count = width // step
    outs, values, gates, _ = expansion_spans(width)
    half = KERNEL // 2
    for tap in range(KERNEL):
        same = masks_seg[:, tap : tap + 1] == seg_rows[...]
        masks[tap] = jnp.broadcast_to(jnp.where(same, 1.0, 0.0), (rows, 128))
    for index, span in enumerate(outs):
        await_columns(matrix, span, sems.at[index])
        added = jnp.dot(context[...], matrix[:, span], preferred_element_type=jnp.float32)
        resid[pl.ds(0, EDGE), span] = added[:EDGE] + low[pl.ds(rows - EDGE, EDGE), span].astype(jnp.float32)
        resid[pl.ds(EDGE, rows), span] = added[EDGE : EDGE + rows] + own[pl.ds(0, rows), span].astype(jnp.float32)
        resid[pl.ds(EDGE + rows, EDGE), span] = added[EDGE + rows :] + up[pl.ds(0, EDGE), span].astype(
            jnp.float32
        )
    conv_in[...] = normalised(resid[...], gain[...])
    for index in range(count):
        await_columns(matrix, values[index], sems.at[count + 2 * index])
        await_columns(matrix, gates[index], sems.at[count + 2 * index + 1])
        value = jnp.dot(conv_in[...], matrix[:, values[index]], preferred_element_type=jnp.float32)
        gate = jnp.dot(conv_in[...], matrix[:, gates[index]], preferred_element_type=jnp.float32)
        glu = (value * jax.nn.sigmoid(gate)).astype(jnp.bfloat16).astype(jnp.float32)
        gated[pl.ds(0, queries), :] = glu
        for shift in range(8):
            moved[shift] = gated[pl.ds(shift, queries), :]

        def lines(group, carry):
            at = pl.multiple_of(group * GROUP, GROUP)
            lanes = range(0, step, 128)
            totals = [jnp.zeros((GROUP, 128), jnp.float32) for _ in lanes]
            for tap in range(KERNEL):
                first = EDGE - half + tap
                mask = masks[tap, pl.ds(at, GROUP), :]
                for number, lane in enumerate(lanes):
                    place = index * step + lane
                    part = moved[first % 8, pl.ds(at + first // 8 * 8, GROUP), lane : lane + 128]
                    totals[number] += part * mask * taps[tap : tap + 1, place : place + 128]
            for total, lane in zip(totals, lanes):
                place = index * step + lane
                act[pl.ds(at, GROUP), place : place + 128] = (total * jax.nn.sigmoid(total)).astype(
                    jnp.bfloat16
                )
            return carry

        lax.fori_loop(0, rows // GROUP, lines, 0)


def convolution(offsets, weight, context, low, own, up, gain, seg_wide, taps):
    rows, width = seg_wide.shape[0] // 3, own.shape[1]
    queries = rows + 2 * EDGE
    step = cut(width, 512)
    whole = pl.BlockSpec(memory_space=pltpu.VMEM)
    first = rows - KERNEL // 2
    seg_taps = jnp.stack([seg_wide[first + tap : first + tap + rows] for tap in range(KERNEL)], axis=1)
    return pl.pallas_call(
        functools.partial(convolution_kernel, len(weight)),
        out_shape=(
            jax.ShapeDtypeStruct((rows, width), jnp.bfloat16),
            jax.ShapeDtypeStruct((rows, width), jnp.float32),
        ),
        in_specs=[pl.BlockSpec(memory_space=pltpu.SMEM)]
        + [whole] * 8
        + [pl.BlockSpec(memory_space=pl.ANY)] * len(weight),
        out_specs=(whole, whole),
        scratch_shapes=[
            pltpu.VMEM((width, 3 * width), jnp.bfloat16),
            pltpu.VMEM((queries, width), jnp.float32),
            pltpu.VMEM((queries, width), jnp.bfloat16),
            pltpu.VMEM((queries + 8, step), jnp.float32),
            pltpu.VMEM((8, queries, step), jnp.float32),
            pltpu.VMEM((KERNEL, rows, 128), jnp.float32),
            pltpu.SemaphoreType.DMA((3 * width // step,)),
        ],
        compiler_params=pltpu.CompilerParams(vmem_limit_bytes=VMEM_BYTES),
        cost_estimate=pl.CostEstimate(
            flops=6 * width * width * queries + 3 * KERNEL * rows * width,
            bytes_accessed=6 * width * width + 8 * rows * width,
            transcendentals=2 * rows * width,
        ),
        name="convolution",
    )(
        offsets, context, low, own, up, gain, seg_wide[rows : 2 * rows][:, None], seg_taps, taps, *weight
    )


def mixing_kernel(pieces, offsets, act, resid, *rest):
    weight, (out, matrix, sems) = rest[:pieces], rest[pieces:]
    width = act.shape[1]
    step = cut(width, 512)
    spans = [pl.ds(at, step) for at in range(0, width, step)]
    for index, span in enumerate(spans):
        load_columns(offsets, weight, matrix, span, sems.at[index])
    for index, span in enumerate(spans):
        await_columns(matrix, span, sems.at[index])
        made = jnp.dot(act[...], matrix[:, span], preferred_element_type=jnp.float32)
        out[:, span] = (resid[:, span] + made).astype(jnp.bfloat16)


def mixing(offsets, weight, act, resid):
    rows, width = act.shape
    whole = pl.BlockSpec(memory_space=pltpu.VMEM)
    return pl.pallas_call(
        functools.partial(mixing_kernel, len(weight)),
        out_shape=jax.ShapeDtypeStruct((rows, width), jnp.bfloat16),
        in_specs=[pl.BlockSpec(memory_space=pltpu.SMEM)]
        + [whole] * 2
        + [pl.BlockSpec(memory_space=pl.ANY)] * len(weight),
        out_specs=whole,
        scratch_shapes=[
            pltpu.VMEM((width, width), jnp.bfloat16),
            pltpu.SemaphoreType.DMA((width // cut(width, 512),)),
        ],
        compiler_params=pltpu.CompilerParams(vmem_limit_bytes=VMEM_BYTES),
        cost_estimate=pl.CostEstimate(
            flops=2 * width * width * rows, bytes_accessed=2 * width * width + 8 * rows * width, transcendentals=0
        ),
        name="mixing",
    )(offsets, act, resid, *weight)


def tick_kernel(counts, offsets, low, own, up, gain_a, gain_c, seg_queries, seg_keys, seg_rows, masks_seg, taps, *rest):
    first, second, third = counts
    qkv, rest = rest[:first], rest[first:]
    expand, rest = rest[:second], rest[second:]
    mix, rest = rest[:third], rest[third:]
    out, context, matrix, normed, query, keys, values, bias, sems, act, expansion, resid, *scratch, mix_sems = rest
    rows, width = out.shape
    step = cut(width, 512)
    spans = [pl.ds(at, step) for at in range(0, width, step)]

    def ask_for_mix():
        for index, span in enumerate(spans):
            load_columns(offsets, mix, matrix, span, mix_sems.at[index])

    attend(
        offsets, qkv, low, own, up, gain_a, seg_queries, seg_keys,
        context, matrix, normed, query, keys, values, bias, sems,
        lambda: ask_for_expansion(offsets, expand, expansion, scratch[-1]), ask_for_mix,
    )
    convolve(context, low, own, up, gain_c, seg_rows, masks_seg, taps, act, expansion, resid, *scratch)
    for index, span in enumerate(spans):
        await_columns(matrix, span, mix_sems.at[index])
        made = jnp.dot(act[...], matrix[:, span], preferred_element_type=jnp.float32)
        out[:, span] = (resid[pl.ds(EDGE, rows), span] + made).astype(jnp.bfloat16)


def whole_tick(offsets, qkv, expand, mix, low, own, up, gain_a, gain_c, seg_wide, taps):
    rows, width = seg_wide.shape[0] // 3, own.shape[1]
    wide, queries, step = 3 * rows, rows + 2 * EDGE, cut(width, 512)
    whole = pl.BlockSpec(memory_space=pltpu.VMEM)
    first = rows - KERNEL // 2
    seg_taps = jnp.stack([seg_wide[first + tap : first + tap + rows] for tap in range(KERNEL)], axis=1)
    pieces = (*qkv, *expand, *mix)
    return pl.pallas_call(
        functools.partial(tick_kernel, (len(qkv), len(expand), len(mix))),
        out_shape=jax.ShapeDtypeStruct((rows, width), jnp.bfloat16),
        in_specs=[pl.BlockSpec(memory_space=pltpu.SMEM)]
        + [whole] * 10
        + [pl.BlockSpec(memory_space=pl.ANY)] * len(pieces),
        out_specs=whole,
        scratch_shapes=[
            pltpu.VMEM((queries, width), jnp.bfloat16),
            pltpu.VMEM((width, 3 * width), jnp.bfloat16),
            pltpu.VMEM((wide, width), jnp.bfloat16),
            pltpu.VMEM((queries, width), jnp.bfloat16),
            pltpu.VMEM((wide, width), jnp.bfloat16),
            pltpu.VMEM((wide, width), jnp.bfloat16),
            pltpu.VMEM((2, queries, 2 * rows + 128), jnp.float32),
            pltpu.SemaphoreType.DMA((3 * width // cut(width, 768),)),
            pltpu.VMEM((rows, width), jnp.bfloat16),
            pltpu.VMEM((width, 3 * width), jnp.bfloat16),
            pltpu.VMEM((queries, width), jnp.float32),
            pltpu.VMEM((queries, width), jnp.bfloat16),
            pltpu.VMEM((queries + 8, step), jnp.float32),
            pltpu.VMEM((8, queries, step), jnp.float32),
            pltpu.VMEM((KERNEL, rows, 128), jnp.float32),
            pltpu.SemaphoreType.DMA((3 * width // step,)),
            pltpu.SemaphoreType.DMA((width // step,)),
        ],
        compiler_params=pltpu.CompilerParams(vmem_limit_bytes=TICK_VMEM_BYTES),
        cost_estimate=pl.CostEstimate(
            flops=2 * width * width * (5 * queries + 2 * wide), bytes_accessed=14 * width * width, transcendentals=0
        ),
        name="tick",
    )(
        offsets, low, own, up, gain_a, gain_c,
        seg_wide[rows - EDGE : 2 * rows + EDGE][:, None], seg_wide[None, :],
        seg_wide[rows : 2 * rows][:, None], seg_taps, taps, *pieces,
    )


def on_device(
    layout,
    newcomer_groups,
    pending_inputs,
    speaker_clip_ids,
    selfattend_scaling,
    triple_projection_matrix,
    selfattend_final_matrix,
    depthwise_scaling,
    sigmoid_expand_matrix,
    filter_taps,
    combine_channel_matrix,
):
    core = lax.axis_index("section") % 2
    high = lax.axis_index("frame") // layout.half
    section = lax.axis_index("section") // 2 * 2 + high
    sections = layout.sections
    ticks = newcomer_groups.shape[0] + 1

    rows, width = pending_inputs.shape[1:]
    batches = speaker_clip_ids.shape[0]
    weights = Weights(layout)
    offsets = weights.offsets(combine_channel_matrix.shape[1])

    small = jnp.concatenate([selfattend_scaling, depthwise_scaling, filter_taps[0]], axis=0)
    small = jnp.where(core == high, small, send(small, layout.flipped(1, 0)))
    gain_a, gain_c, taps = small[0:1], small[1:2], small[2:]

    ids = (speaker_clip_ids + 1).astype(jnp.bfloat16)
    ids = jnp.pad(ids, ((0, -batches % 16), (0, width - rows)))
    own_1 = weights.to_half(behind(triple_projection_matrix[0], small))
    packed = jnp.concatenate([pending_inputs[0], ids], axis=0)
    packed = send(behind(packed, own_1), layout.to_workers())
    expand = jnp.concatenate([selfattend_final_matrix[0], sigmoid_expand_matrix[0]], axis=1)
    own_2 = weights.to_half(behind(expand, own_1))
    own_3 = weights.to_half(behind(combine_channel_matrix[0], own_2))
    sides_1 = weights.to_sides(own_1)
    sides_2 = weights.to_sides(behind(own_2, sides_1))
    packed_out = behind(packed, sides_1)
    packed = (send(packed_out, layout.shifted(1)), packed, send(packed_out, layout.shifted(-1)))
    diagonal_1 = weights.to_diagonal(*sides_1, False)
    qkv = weights.whole(own_1, sides_1, diagonal_1, packed, own_3)
    packed = behind(packed, own_3)

    ids = jnp.concatenate([part[rows : rows + batches, :rows] for part in packed], axis=1)
    ids = ids.astype(jnp.int32)
    low, present, up = packed

    made_all = []
    for tick in range(ticks):
        batch = sections - 1 - section + tick
        seg_wide = lax.dynamic_index_in_dim(ids, batch, 0, keepdims=False)
        if tick > 0:
            made = whole_tick(offsets, qkv, out_expand, mix, low, present, up, gain_a, gain_c, seg_wide, taps)
        else:
            context = attention(offsets, qkv, low, present, up, gain_a, seg_wide)
            diagonal_2 = weights.to_diagonal(*behind(sides_2, context), True)
            sides_3 = weights.to_sides(behind(own_3, sides_2, context))
            out_expand = weights.whole_by_parts(own_2, sides_2, diagonal_2, context)
            diagonal_3 = weights.to_diagonal(*behind(sides_3, diagonal_2), True)
            newcomers = behind(newcomer_groups, diagonal_2)
            newcomers = [send(newcomers[coming], layout.first()) for coming in range(ticks - 1)]
            act, resid = convolution(offsets, out_expand, context, low, present, up, gain_c, seg_wide, taps)
            mix = weights.whole(own_3, sides_3, diagonal_3, act)
            made = mixing(offsets, mix, act, resid)
        made_all.append(send(made, layout.to_homes()))
        if tick + 1 < ticks:
            arrived = send(made, layout.relay())
            present = jnp.where(section == 0, newcomers[tick], arrived)
            low, up = send(present, layout.shifted(1)), send(present, layout.shifted(-1))
    return jnp.stack(made_all)[:, None]


def solution(mesh):
    layout = Layout(mesh.shape["section"], mesh.shape["frame"])
    in_specs = (
        P(None, "frame", None),
        P("section", "frame", None),
        P(None, "frame"),
        P("section", None),
        P("section", "frame", None),
        P("section", "frame", None),
        P("section", None),
        P("section", "frame", None),
        P("section", None, None),
        P("section", "frame", None),
    )
    out_specs = P(None, "section", "frame", None)

    def local(*args):
        return on_device(layout, *args)

    return jax.shard_map(
        local, mesh=mesh, in_specs=in_specs, out_specs=out_specs, check_vma=False
    )
```

```python
import functools

import jax
import jax.numpy as jnp
from jax import lax
from jax.experimental import pallas as pl
from jax.experimental.pallas import tpu as pltpu
from jax.sharding import PartitionSpec as P

HEADS = 24
KERNEL = 31
EPS = 1e-05
EDGE = 16
GROUP = 32
VMEM_BYTES = 56 * 1024 * 1024
TICK_VMEM_BYTES = 60 * 1024 * 1024
AXES = ("section", "frame")


class Layout:
    def __init__(self, sections, frames):
        self.sections, self.frames, self.half = sections, frames, frames // 2
        self.gray = [r ^ (r >> 1) for r in range(self.half)]
        if sorted(self.gray) != list(range(self.half)):
            self.gray = list(range(self.half))

    def flat(self, section, frame):
        return section * self.frames + frame

    def worker(self, section, block):
        pair, high = divmod(section, 2)
        return self.flat(2 * pair + block % 2, high * self.half + self.gray.index(block // 2))

    def each(self):
        return [(s, b) for s in range(self.sections) for b in range(self.frames)]

    def to_workers(self, step=0):
        return [
            (self.flat(s, b + step), self.worker(s, b))
            for s, b in self.each()
            if 0 <= b + step < self.frames
        ]

    def to_homes(self):
        return [(there, here) for here, there in self.to_workers()]

    def shifted(self, step):
        return [
            (self.worker(s, b), self.worker(s, b + step))
            for s, b in self.each()
            if 0 <= b + step < self.frames
        ]

    def relay(self):
        return [
            (self.worker(s, b), self.worker(s + 1, b)) for s, b in self.each() if s + 1 < self.sections
        ]

    def first(self):
        return [(self.flat(0, b), self.worker(0, b)) for b in range(self.frames)]

    def rows_to_half(self):
        moves = []
        for s, f in self.each():
            (pair, high), (core, rest) = divmod(s, 2), divmod(f, self.half)
            if core != high:
                moves.append((self.flat(s, f), self.flat(2 * pair + core, high * self.half + rest)))
        return moves

    def flipped(self, section_bit, frame_bits):
        return [(self.flat(s, f), self.flat(s ^ section_bit, f ^ frame_bits)) for s, f in self.each()]

    def diagonal(self):
        return [
            (self.flat(s, f), self.flat(s, f ^ (1 if s % 2 == f // self.half else 2)))
            for s, f in self.each()
        ]

    def groups(self):
        return [
            [self.flat(2 * k + c, h * self.half + r) for c in range(2) for r in range(self.half)]
            for k in range(self.sections // 2)
            for h in range(2)
        ]


def send(value, moves):
    return lax.ppermute(value, AXES, moves)


def behind(value, *earlier):
    return lax.optimization_barrier((value, earlier))[0]


class Weights:
    def __init__(self, layout):
        self.layout = layout
        self.core = lax.axis_index("section") % 2
        self.rest = lax.axis_index("frame") % layout.half
        self.at_home = self.core == lax.axis_index("frame") // layout.half
        self.tree = layout.half == 4

    def to_half(self, chunk):
        return jnp.where(self.at_home, chunk, send(chunk, self.layout.rows_to_half()))

    def to_sides(self, own):
        if not self.tree:
            return own, own
        return send(own, self.layout.flipped(0, 1)), send(own, self.layout.flipped(0, 2))

    def to_diagonal(self, along_x, along_z, even):
        if not self.tree:
            return along_x, along_z
        half = along_x.shape[1] // 2
        low = send(along_z[:, :half], self.layout.flipped(0, 1))
        if even:
            return low, send(along_x[:, half:], self.layout.flipped(0, 2))
        high = jnp.where(self.at_home, along_z[:, half:], along_x[:, half:])
        return low, send(high, self.layout.diagonal())

    def offsets(self, rows):
        if not self.tree:
            return jnp.zeros((1,), jnp.int32)
        near = self.core * 4 + (jnp.arange(4) ^ self.rest)
        return jnp.concatenate([near, near ^ 4]).astype(jnp.int32) * rows

    def whole(self, own, sides, diagonal, *earlier):
        if not self.tree:
            whole = lax.all_gather(
                own, AXES, axis=0, tiled=True, axis_index_groups=self.layout.groups()
            )
            return (whole[None],)
        own, sides, diagonal = behind((own, sides, diagonal), *earlier)
        near = jnp.stack([own, *sides, jnp.concatenate(diagonal, axis=1)])
        return near, send(near, self.layout.flipped(1, 0))

    def whole_by_parts(self, own, sides, diagonal, *earlier):
        if not self.tree:
            return self.whole(own, sides, diagonal)
        own, sides = behind((own, sides), *earlier)
        near = jnp.stack([own, *sides])
        far = send(near, self.layout.flipped(1, 0))
        last = jnp.concatenate(diagonal, axis=1)[None]
        return near, last, far, send(last, self.layout.flipped(1, 0))


def cut(total, most):
    return max(w for w in range(128, most + 1, 128) if total % w == 0)


def load_columns(offsets, pieces, target, columns, sem):
    place = 0
    for piece in pieces:
        count, height = piece.shape[:2]
        for index in range(count):
            row = pl.multiple_of(offsets[place], 16)
            place += 1
            pltpu.make_async_copy(
                piece.at[index, :, columns], target.at[pl.ds(row, height), columns], sem
            ).start()


def await_columns(target, columns, sem):
    pltpu.make_async_copy(target.at[:, columns], target.at[:, columns], sem).wait()


def normalised(lines, gain):
    mean = jnp.mean(lines, axis=-1, keepdims=True)
    centred = lines - mean
    spread = jnp.mean(centred * centred, axis=-1, keepdims=True)
    return (centred * lax.rsqrt(spread + EPS) * gain).astype(jnp.bfloat16)


def attention_kernel(pieces, offsets, low, own, up, gain, seg_rows, seg_keys, *rest):
    attend(offsets, rest[:pieces], low, own, up, gain, seg_rows, seg_keys, *rest[pieces:])


def attend(
    offsets, weight, low, own, up, gain, seg_rows, seg_keys,
    context, matrix, normed, query, keys, values, bias, sems, asked_all=None, projected=None,
):
    queries, width = context.shape
    rows = queries - 2 * EDGE
    wide, start = 3 * rows, rows - EDGE
    step = cut(width, 768)
    spans = [pl.ds(at, step) for at in range(0, 3 * width, step)]
    for index, span in enumerate(spans):
        load_columns(offsets, weight, matrix, span, sems.at[index])
    if asked_all is not None:
        asked_all()
    for index, block in enumerate((low, own, up)):
        normed[pl.ds(index * rows, rows), :] = normalised(
            block[pl.ds(0, rows), :].astype(jnp.float32), gain[...]
        )
    tile, window = queries // 2, 2 * rows + 128
    firsts = (0, wide - window)
    for part in range(2):
        same = seg_rows[pl.ds(part * tile, tile), :] == seg_keys[:, pl.ds(firsts[part], window)]
        sheet = jnp.where(same, 0.0, -1e30)
        bias[part, pl.ds(0, tile), :] = sheet
        bias[part, pl.ds(tile, tile), :] = sheet
    per = width // step
    for index, span in enumerate(spans):
        await_columns(matrix, span, sems.at[index])
        kind, at = divmod(index, per)
        place = pl.ds(at * step, step)
        if kind == 0:
            made = jnp.dot(
                normed[pl.ds(start, queries), :], matrix[:, span], preferred_element_type=jnp.float32
            )
            query[:, place] = (made * (width // HEADS) ** (-0.5)).astype(jnp.bfloat16)
        else:
            made = jnp.dot(normed[...], matrix[:, span], preferred_element_type=jnp.float32)
            (keys if kind == 1 else values)[:, place] = made.astype(jnp.bfloat16)

    if projected is not None:
        projected()
    head = width // HEADS
    together = 128 // head
    lanes = lax.broadcasted_iota(jnp.int32, (tile, 128), 1) // head
    ones = jnp.ones((window, 128), jnp.bfloat16)

    def heads(index, carry):
        place = pl.ds(pl.multiple_of(index * 128, 128), 128)
        for part in range(2):
            asked = query[pl.ds(part * tile, tile), place]
            stacked = jnp.concatenate(
                [jnp.where(lanes == one, asked, jnp.zeros_like(asked)) for one in range(together)], axis=0
            )
            seen = pl.ds(firsts[part], window)
            scores = lax.dot_general(
                stacked, keys[seen, place], (((1,), (1,)), ((), ())), preferred_element_type=jnp.float32
            )
            scores = scores + bias[part]
            expd = jnp.exp(scores - jnp.max(scores, axis=-1, keepdims=True))
            shown = jnp.concatenate([values[seen, place], ones], axis=1)
            mixed = jnp.dot(expd.astype(jnp.bfloat16), shown, preferred_element_type=jnp.float32)
            mixed = mixed[:, :128] / mixed[:, 128:]
            result = mixed[:tile]
            for one in range(1, together):
                result = jnp.where(lanes == one, mixed[one * tile : (one + 1) * tile], result)
            context[pl.ds(part * tile, tile), place] = result.astype(jnp.bfloat16)
        return carry

    lax.fori_loop(0, width // 128, heads, 0, unroll=2)


def attention(offsets, weight, low, own, up, gain, seg_wide):
    rows, width = seg_wide.shape[0] // 3, own.shape[1]
    wide, queries = 3 * rows, rows + 2 * EDGE
    spans = 3 * width // cut(width, 768)
    whole = pl.BlockSpec(memory_space=pltpu.VMEM)
    seg_rows = seg_wide[rows - EDGE : 2 * rows + EDGE][:, None]
    return pl.pallas_call(
        functools.partial(attention_kernel, len(weight)),
        out_shape=jax.ShapeDtypeStruct((queries, width), jnp.bfloat16),
        in_specs=[pl.BlockSpec(memory_space=pltpu.SMEM)]
        + [whole] * 6
        + [pl.BlockSpec(memory_space=pl.ANY)] * len(weight),
        out_specs=whole,
        scratch_shapes=[
            pltpu.VMEM((width, 3 * width), jnp.bfloat16),
            pltpu.VMEM((wide, width), jnp.bfloat16),
            pltpu.VMEM((queries, width), jnp.bfloat16),
            pltpu.VMEM((wide, width), jnp.bfloat16),
            pltpu.VMEM((wide, width), jnp.bfloat16),
            pltpu.VMEM((2, queries, 2 * rows + 128), jnp.float32),
            pltpu.SemaphoreType.DMA((spans,)),
        ],
        compiler_params=pltpu.CompilerParams(vmem_limit_bytes=VMEM_BYTES),
        cost_estimate=pl.CostEstimate(
            flops=2 * width * width * (queries + 2 * wide) + 4 * queries * wide * width,
            bytes_accessed=6 * width * width + 8 * rows * width,
            transcendentals=HEADS * queries * wide,
        ),
        name="attention",
    )(offsets, low, own, up, gain, seg_rows, seg_wide[None, :], *weight)


def convolution_kernel(
    pieces, offsets, context, low, own, up, gain, seg_rows, masks_seg, taps, *rest
):
    weight, (act, resid_out, matrix, resid, *scratch) = rest[:pieces], rest[pieces:]
    ask_for_expansion(offsets, weight, matrix, scratch[-1])
    convolve(context, low, own, up, gain, seg_rows, masks_seg, taps, act, matrix, resid, *scratch)
    resid_out[...] = resid[pl.ds(EDGE, act.shape[0]), :]


def expansion_spans(width):
    step = cut(width, 512)
    outs, values, gates = (
        [pl.ds(part * width + at, step) for at in range(0, width, step)] for part in range(3)
    )
    return outs, values, gates, outs + [span for both in zip(values, gates) for span in both]


def ask_for_expansion(offsets, weight, matrix, sems):
    for index, span in enumerate(expansion_spans(matrix.shape[0])[3]):
        load_columns(offsets, weight, matrix, span, sems.at[index])


def convolve(
    context, low, own, up, gain, seg_rows, masks_seg, taps, act, matrix, resid, conv_in, gated, moved, masks, sems
):
    rows, width = act.shape
    queries = rows + 2 * EDGE
    step = cut(width, 512)
    count = width // step
    outs, values, gates, _ = expansion_spans(width)
    half = KERNEL // 2
    for tap in range(KERNEL):
        same = masks_seg[:, tap : tap + 1] == seg_rows[...]
        masks[tap] = jnp.broadcast_to(jnp.where(same, 1.0, 0.0), (rows, 128))
    for index, span in enumerate(outs):
        await_columns(matrix, span, sems.at[index])
        added = jnp.dot(context[...], matrix[:, span], preferred_element_type=jnp.float32)
        resid[pl.ds(0, EDGE), span] = added[:EDGE] + low[pl.ds(rows - EDGE, EDGE), span].astype(jnp.float32)
        resid[pl.ds(EDGE, rows), span] = added[EDGE : EDGE + rows] + own[pl.ds(0, rows), span].astype(jnp.float32)
        resid[pl.ds(EDGE + rows, EDGE), span] = added[EDGE + rows :] + up[pl.ds(0, EDGE), span].astype(
            jnp.float32
        )
    conv_in[...] = normalised(resid[...], gain[...])
    for index in range(count):
        await_columns(matrix, values[index], sems.at[count + 2 * index])
        await_columns(matrix, gates[index], sems.at[count + 2 * index + 1])
        value = jnp.dot(conv_in[...], matrix[:, values[index]], preferred_element_type=jnp.float32)
        gate = jnp.dot(conv_in[...], matrix[:, gates[index]], preferred_element_type=jnp.float32)
        glu = (value * jax.nn.sigmoid(gate)).astype(jnp.bfloat16).astype(jnp.float32)
        gated[pl.ds(0, queries), :] = glu
        for shift in range(8):
            moved[shift] = gated[pl.ds(shift, queries), :]

        def lines(group, carry):
            at = pl.multiple_of(group * GROUP, GROUP)
            lanes = range(0, step, 128)
            totals = [jnp.zeros((GROUP, 128), jnp.float32) for _ in lanes]
            for tap in range(KERNEL):
                first = EDGE - half + tap
                mask = masks[tap, pl.ds(at, GROUP), :]
                for number, lane in enumerate(lanes):
                    place = index * step + lane
                    part = moved[first % 8, pl.ds(at + first // 8 * 8, GROUP), lane : lane + 128]
                    totals[number] += part * mask * taps[tap : tap + 1, place : place + 128]
            for total, lane in zip(totals, lanes):
                place = index * step + lane
                act[pl.ds(at, GROUP), place : place + 128] = (total * jax.nn.sigmoid(total)).astype(
                    jnp.bfloat16
                )
            return carry

        lax.fori_loop(0, rows // GROUP, lines, 0)


def convolution(offsets, weight, context, low, own, up, gain, seg_wide, taps):
    rows, width = seg_wide.shape[0] // 3, own.shape[1]
    queries = rows + 2 * EDGE
    step = cut(width, 512)
    whole = pl.BlockSpec(memory_space=pltpu.VMEM)
    first = rows - KERNEL // 2
    seg_taps = jnp.stack([seg_wide[first + tap : first + tap + rows] for tap in range(KERNEL)], axis=1)
    return pl.pallas_call(
        functools.partial(convolution_kernel, len(weight)),
        out_shape=(
            jax.ShapeDtypeStruct((rows, width), jnp.bfloat16),
            jax.ShapeDtypeStruct((rows, width), jnp.float32),
        ),
        in_specs=[pl.BlockSpec(memory_space=pltpu.SMEM)]
        + [whole] * 8
        + [pl.BlockSpec(memory_space=pl.ANY)] * len(weight),
        out_specs=(whole, whole),
        scratch_shapes=[
            pltpu.VMEM((width, 3 * width), jnp.bfloat16),
            pltpu.VMEM((queries, width), jnp.float32),
            pltpu.VMEM((queries, width), jnp.bfloat16),
            pltpu.VMEM((queries + 8, step), jnp.float32),
            pltpu.VMEM((8, queries, step), jnp.float32),
            pltpu.VMEM((KERNEL, rows, 128), jnp.float32),
            pltpu.SemaphoreType.DMA((3 * width // step,)),
        ],
        compiler_params=pltpu.CompilerParams(vmem_limit_bytes=VMEM_BYTES),
        cost_estimate=pl.CostEstimate(
            flops=6 * width * width * queries + 3 * KERNEL * rows * width,
            bytes_accessed=6 * width * width + 8 * rows * width,
            transcendentals=2 * rows * width,
        ),
        name="convolution",
    )(
        offsets, context, low, own, up, gain, seg_wide[rows : 2 * rows][:, None], seg_taps, taps, *weight
    )


def mixing_kernel(pieces, offsets, act, resid, *rest):
    weight, (out, matrix, sems) = rest[:pieces], rest[pieces:]
    width = act.shape[1]
    step = cut(width, 512)
    spans = [pl.ds(at, step) for at in range(0, width, step)]
    for index, span in enumerate(spans):
        load_columns(offsets, weight, matrix, span, sems.at[index])
    for index, span in enumerate(spans):
        await_columns(matrix, span, sems.at[index])
        made = jnp.dot(act[...], matrix[:, span], preferred_element_type=jnp.float32)
        out[:, span] = (resid[:, span] + made).astype(jnp.bfloat16)


def mixing(offsets, weight, act, resid):
    rows, width = act.shape
    whole = pl.BlockSpec(memory_space=pltpu.VMEM)
    return pl.pallas_call(
        functools.partial(mixing_kernel, len(weight)),
        out_shape=jax.ShapeDtypeStruct((rows, width), jnp.bfloat16),
        in_specs=[pl.BlockSpec(memory_space=pltpu.SMEM)]
        + [whole] * 2
        + [pl.BlockSpec(memory_space=pl.ANY)] * len(weight),
        out_specs=whole,
        scratch_shapes=[
            pltpu.VMEM((width, width), jnp.bfloat16),
            pltpu.SemaphoreType.DMA((width // cut(width, 512),)),
        ],
        compiler_params=pltpu.CompilerParams(vmem_limit_bytes=VMEM_BYTES),
        cost_estimate=pl.CostEstimate(
            flops=2 * width * width * rows, bytes_accessed=2 * width * width + 8 * rows * width, transcendentals=0
        ),
        name="mixing",
    )(offsets, act, resid, *weight)


def tick_kernel(counts, offsets, low, own, up, gain_a, gain_c, seg_queries, seg_keys, seg_rows, masks_seg, taps, *rest):
    first, second, third = counts
    qkv, rest = rest[:first], rest[first:]
    expand, rest = rest[:second], rest[second:]
    mix, rest = rest[:third], rest[third:]
    out, context, matrix, normed, query, keys, values, bias, sems, act, expansion, resid, *scratch, mix_sems = rest
    rows, width = out.shape
    step = cut(width, 512)
    spans = [pl.ds(at, step) for at in range(0, width, step)]

    def ask_for_mix():
        for index, span in enumerate(spans):
            load_columns(offsets, mix, matrix, span, mix_sems.at[index])

    attend(
        offsets, qkv, low, own, up, gain_a, seg_queries, seg_keys,
        context, matrix, normed, query, keys, values, bias, sems,
        lambda: ask_for_expansion(offsets, expand, expansion, scratch[-1]), ask_for_mix,
    )
    convolve(context, low, own, up, gain_c, seg_rows, masks_seg, taps, act, expansion, resid, *scratch)
    for index, span in enumerate(spans):
        await_columns(matrix, span, mix_sems.at[index])
        made = jnp.dot(act[...], matrix[:, span], preferred_element_type=jnp.float32)
        out[:, span] = (resid[pl.ds(EDGE, rows), span] + made).astype(jnp.bfloat16)


def whole_tick(offsets, qkv, expand, mix, low, own, up, gain_a, gain_c, seg_wide, taps):
    rows, width = seg_wide.shape[0] // 3, own.shape[1]
    wide, queries, step = 3 * rows, rows + 2 * EDGE, cut(width, 512)
    whole = pl.BlockSpec(memory_space=pltpu.VMEM)
    first = rows - KERNEL // 2
    seg_taps = jnp.stack([seg_wide[first + tap : first + tap + rows] for tap in range(KERNEL)], axis=1)
    pieces = (*qkv, *expand, *mix)
    return pl.pallas_call(
        functools.partial(tick_kernel, (len(qkv), len(expand), len(mix))),
        out_shape=jax.ShapeDtypeStruct((rows, width), jnp.bfloat16),
        in_specs=[pl.BlockSpec(memory_space=pltpu.SMEM)]
        + [whole] * 10
        + [pl.BlockSpec(memory_space=pl.ANY)] * len(pieces),
        out_specs=whole,
        scratch_shapes=[
            pltpu.VMEM((queries, width), jnp.bfloat16),
            pltpu.VMEM((width, 3 * width), jnp.bfloat16),
            pltpu.VMEM((wide, width), jnp.bfloat16),
            pltpu.VMEM((queries, width), jnp.bfloat16),
            pltpu.VMEM((wide, width), jnp.bfloat16),
            pltpu.VMEM((wide, width), jnp.bfloat16),
            pltpu.VMEM((2, queries, 2 * rows + 128), jnp.float32),
            pltpu.SemaphoreType.DMA((3 * width // cut(width, 768),)),
            pltpu.VMEM((rows, width), jnp.bfloat16),
            pltpu.VMEM((width, 3 * width), jnp.bfloat16),
            pltpu.VMEM((queries, width), jnp.float32),
            pltpu.VMEM((queries, width), jnp.bfloat16),
            pltpu.VMEM((queries + 8, step), jnp.float32),
            pltpu.VMEM((8, queries, step), jnp.float32),
            pltpu.VMEM((KERNEL, rows, 128), jnp.float32),
            pltpu.SemaphoreType.DMA((3 * width // step,)),
            pltpu.SemaphoreType.DMA((width // step,)),
        ],
        compiler_params=pltpu.CompilerParams(vmem_limit_bytes=TICK_VMEM_BYTES),
        cost_estimate=pl.CostEstimate(
            flops=2 * width * width * (5 * queries + 2 * wide), bytes_accessed=14 * width * width, transcendentals=0
        ),
        name="tick",
    )(
        offsets, low, own, up, gain_a, gain_c,
        seg_wide[rows - EDGE : 2 * rows + EDGE][:, None], seg_wide[None, :],
        seg_wide[rows : 2 * rows][:, None], seg_taps, taps, *pieces,
    )


def on_device(
    layout,
    newcomer_groups,
    pending_inputs,
    speaker_clip_ids,
    selfattend_scaling,
    triple_projection_matrix,
    selfattend_final_matrix,
    depthwise_scaling,
    sigmoid_expand_matrix,
    filter_taps,
    combine_channel_matrix,
):
    core = lax.axis_index("section") % 2
    high = lax.axis_index("frame") // layout.half
    section = lax.axis_index("section") // 2 * 2 + high
    sections = layout.sections
    ticks = newcomer_groups.shape[0] + 1

    rows, width = pending_inputs.shape[1:]
    batches = speaker_clip_ids.shape[0]
    weights = Weights(layout)
    offsets = weights.offsets(combine_channel_matrix.shape[1])

    small = jnp.concatenate([selfattend_scaling, depthwise_scaling, filter_taps[0]], axis=0)
    small = jnp.where(core == high, small, send(small, layout.flipped(1, 0)))
    gain_a, gain_c, taps = small[0:1], small[1:2], small[2:]

    ids = (speaker_clip_ids + 1).astype(jnp.bfloat16)
    ids = jnp.pad(ids, ((0, -batches % 16), (0, width - rows)))
    own_1 = weights.to_half(behind(triple_projection_matrix[0], small))
    packed = jnp.concatenate([pending_inputs[0], ids], axis=0)
    packed = send(behind(packed, own_1), layout.to_workers())
    expand = jnp.concatenate([selfattend_final_matrix[0], sigmoid_expand_matrix[0]], axis=1)
    own_2 = weights.to_half(behind(expand, own_1))
    own_3 = weights.to_half(behind(combine_channel_matrix[0], own_2))
    sides_1 = weights.to_sides(own_1)
    sides_2 = weights.to_sides(behind(own_2, sides_1))
    packed_out = behind(packed, sides_1)
    packed = (send(packed_out, layout.shifted(1)), packed, send(packed_out, layout.shifted(-1)))
    diagonal_1 = weights.to_diagonal(*sides_1, False)
    qkv = weights.whole(own_1, sides_1, diagonal_1, packed, own_3)
    packed = behind(packed, own_3)

    ids = jnp.concatenate([part[rows : rows + batches, :rows] for part in packed], axis=1)
    ids = ids.astype(jnp.int32)
    low, present, up = packed

    made_all = []
    for tick in range(ticks):
        batch = sections - 1 - section + tick
        seg_wide = lax.dynamic_index_in_dim(ids, batch, 0, keepdims=False)
        if tick > 0:
            made = whole_tick(offsets, qkv, out_expand, mix, low, present, up, gain_a, gain_c, seg_wide, taps)
        else:
            context = attention(offsets, qkv, low, present, up, gain_a, seg_wide)
            diagonal_2 = weights.to_diagonal(*behind(sides_2, context), True)
            sides_3 = weights.to_sides(behind(own_3, sides_2, context))
            out_expand = weights.whole_by_parts(own_2, sides_2, diagonal_2, context)
            diagonal_3 = weights.to_diagonal(*behind(sides_3, diagonal_2), True)
            newcomers = behind(newcomer_groups, diagonal_2)
            newcomers = [send(newcomers[coming], layout.first()) for coming in range(ticks - 1)]
            act, resid = convolution(offsets, out_expand, context, low, present, up, gain_c, seg_wide, taps)
            mix = weights.whole(own_3, sides_3, diagonal_3, act)
            made = mixing(offsets, mix, act, resid)
        if tick + 1 < ticks:
            arrived = send(made, layout.relay())
            present = jnp.where(section == 0, newcomers[tick], arrived)
            low, up = send(present, layout.shifted(1)), send(present, layout.shifted(-1))
            made = behind(made, low, up)
        made_all.append(send(made, layout.to_homes()))
    return jnp.stack(made_all)[:, None]


def solution(mesh):
    layout = Layout(mesh.shape["section"], mesh.shape["frame"])
    in_specs = (
        P(None, "frame", None),
        P("section", "frame", None),
        P(None, "frame"),
        P("section", None),
        P("section", "frame", None),
        P("section", "frame", None),
        P("section", None),
        P("section", "frame", None),
        P("section", None, None),
        P("section", "frame", None),
    )
    out_specs = P(None, "section", "frame", None)

    def local(*args):
        return on_device(layout, *args)

    return jax.shard_map(
        local, mesh=mesh, in_specs=in_specs, out_specs=out_specs, check_vma=False
    )
```
